256 devices in a mesh: dp: 64 (over z, y, core), feat: 4 (over x).
Axes of the slice: x: 4, y: 4, z: 8, core: 2. Of those that a mesh axis runs over, the one named last changes fastest.
Arguments:
- embeddings: bfloat16 [65536, 512], P('dp', 'feat'), may hold values from -6 to 6
- code_ids: int32 [3, 65536], P(None, 'dp'), may hold values from 0 to 8191, as said below
- codebooks: float32 [3, 8192, 512], P(None, 'dp', 'feat'), may hold values from -4 to 4
- item_weight: bfloat16 [65536], P('dp'), may hold values from 0.25 to 4
Outputs:
- updated_books: float32 [3, 8192, 512], P(None, 'dp', 'feat')
- final_residual: bfloat16 [65536, 512], P('dp', 'feat')
- item_error: float32 [65536], P('dp')
The draws below stay inside these ranges and needn't reach their ends.
Inputs may be any that keep to these rules, and one draw needn't show every extreme that they name: `code_ids`: codes k with o * 128 <= k < (o + 1) * 128 form run o. In each section, each aligned block of 1024 items holds at most 32 items whose codes lie in one run, and in every section some run receives exactly 32 items from every block.
All inputs are finite; a program needn't handle non-finite values.
Results may differ from the reference program's by a relative error of at most 0.0057.
Values may be sent and summed in bfloat16 or wider, within the bound.
No kernel may reach another device: no remote copies, remote signals or barrier semaphores. Data moves between devices by JAX's collectives and lax.ppermute only.
A program may use at most 64 MiB of HBM per device.

```python
import math
import jax
import jax.numpy as jnp

DIM = 512
CODES = 8192
SECTIONS = 3
ITEMS_DEV = 1024
ITEMS = 65536
CODES_OWN = 128
CAP = 32


def block_codes(key, heavy):
    owners_count = CODES // CODES_OWN
    slots = owners_count * CAP
    first_key, second_key, third_key = jax.random.split(key, 3)
    ranks = jax.random.permutation(first_key, slots).astype(jnp.int32)
    slot_ids = jnp.arange(slots, dtype=jnp.int32)
    slot_owner = slot_ids // CAP
    scores = jnp.where(slot_owner == heavy, slot_ids - slots, ranks)
    order = jnp.argsort(scores, stable=True)
    chosen = order[:ITEMS_DEV] // CAP
    shuffle = jax.random.permutation(second_key, ITEMS_DEV)
    owners = chosen[shuffle].astype(jnp.int32)
    local_ids = jax.random.randint(third_key, (ITEMS_DEV,), 0, CODES_OWN, dtype=jnp.int32)
    return owners * CODES_OWN + local_ids


def section_codes(key):
    owners_count = CODES // CODES_OWN
    heavy_key, block_key = jax.random.split(key)
    heavy = jax.random.randint(heavy_key, (), 0, owners_count, dtype=jnp.int32)
    block_keys = jax.random.split(block_key, ITEMS // ITEMS_DEV)
    blocks = jax.vmap(lambda single: block_codes(single, heavy))(block_keys)
    return blocks.reshape(ITEMS)


def draw_code_ids(key, part):
    key = jax.random.fold_in(key, 11)
    section_keys = jax.random.split(key, SECTIONS)
    return jax.vmap(section_codes)(section_keys).astype(jnp.int32)


def level_of(rng, extent, pieces, least, largest):
    loudness = 1.0
    for dim, shards_of in pieces:
        draws = jax.random.uniform(jax.random.fold_in(jax.random.fold_in(rng, 6), dim), (shards_of,), jnp.float32, least / len(pieces), largest / len(pieces))
        loudness = loudness * jnp.repeat(jnp.exp(draws), extent[dim] // shards_of).reshape((-1,) + (1,) * (len(extent) - 1 - dim))
    return loudness


def centred(rng, dims, width, reach, cuts=(), kind=jnp.bfloat16):
    level = level_of(rng, dims, cuts, -0.22, 0.18) if cuts else 1.0
    drawn = jax.random.normal(rng, dims, jnp.float32) * width * level
    return jnp.minimum(jnp.maximum(drawn, -reach), reach).astype(kind)


def setup_inputs(seed: int = 0) -> dict:
    splits = jax.random.split(jax.random.key(seed), 5)
    embeddings = centred(splits[0], (ITEMS, DIM), 1.0, 6.0, ((0, 64), (1, 4)))
    code_ids = draw_code_ids(jax.random.fold_in(splits[4], 71), 0)
    codebooks = centred(splits[2], (SECTIONS, CODES, DIM), 0.5, 4.0, ((1, 64), (2, 4)), jnp.float32)
    item_weight = jnp.clip(jnp.exp(math.log(4.0) - 2.7725887 * jax.random.uniform(splits[3], (ITEMS,), jnp.float32) ** level_of(splits[3], (ITEMS,), ((0, 64),), -0.2, 0.2)), 0.25, 4.0).astype(jnp.bfloat16)
    return {"embeddings": embeddings, "code_ids": code_ids, "codebooks": codebooks, "item_weight": item_weight}


prior_weight = 4.0


def reference(embeddings, code_ids, codebooks, item_weight):
    residual = embeddings
    weights_wide = item_weight.astype(jnp.float32)
    updated_all = []
    for section_idx in range(SECTIONS):
        codes_now = code_ids[section_idx].astype(jnp.int32)
        weighted = residual.astype(jnp.float32) * weights_wide[:, None]
        code_sums = jax.ops.segment_sum(weighted, codes_now, num_segments=CODES)
        counts = jax.ops.segment_sum(weights_wide, codes_now, num_segments=CODES)
        updated = (prior_weight * codebooks[section_idx] + code_sums) / (prior_weight + counts)[:, None]
        updated_all.append(updated)
        residual = (residual.astype(jnp.float32) - updated[codes_now]).astype(jnp.bfloat16)
    wide = residual.astype(jnp.float32)
    item_error = jnp.sum(wide * wide, axis=1)
    return jnp.stack(updated_all), residual, item_error
```

```python
import jax
import jax.numpy as jnp
from jax import lax
from jax.experimental import pallas as pl
from jax.experimental.pallas import tpu as pltpu
from jax.sharding import PartitionSpec as P

F32 = jnp.float32
BF16 = jnp.bfloat16
SECTIONS = 3
RUNS = 64
BLOCKS = 64
FEATS = 128
prior_weight = 4.0

ROWS_IN = 64
ROWS_OUT = 32


def two_parts(x):
    head = x.astype(BF16).astype(F32)
    return head, x - head


def pack_kernel(emb_ref, ids_ref, w_ref, book_ref, out_ref, emb_rows, book_rows):
    for block in range(8):
        turned = emb_ref[block * 128 : (block + 1) * 128, :].astype(F32).T
        for group in range(16):
            which, first = group // 8, (group % 8) * 8
            emb_rows[pl.ds(first * 16 + which * 8 + block, 8, stride=16), :] = turned[
                group * 8 : (group + 1) * 8
            ]
    book_rows[...] = jnp.zeros_like(book_rows)
    for section in range(SECTIONS):
        parts = two_parts(book_ref[section].T)
        for part in range(2):
            for group in range(16):
                which, first = group // 8, (group % 8) * 8
                book_rows[
                    pl.ds(first * 16 + part * 8 + section * 2 + which, 8, stride=16), :
                ] = parts[part][group * 8 : (group + 1) * 8]
    ids = ids_ref[...]
    run = ids >> 7
    coded = ((ids & 127) + 128).astype(F32)
    for bit in range(6):
        coded = coded * jnp.where((run >> bit) & 1 == 1, 2.0 ** (1 << bit), 1.0)
    shared = jnp.concatenate([coded, w_ref[...].astype(F32)], axis=0).astype(BF16)

    @pl.loop(0, RUNS)
    def _(dest):
        out_ref[dest, 0:16, :] = emb_rows[pl.ds(pl.multiple_of(dest * 16, 16), 16), :].astype(BF16)
        out_ref[dest, 16:48, :] = shared
        out_ref[dest, 48:64, :] = book_rows[pl.ds(pl.multiple_of(dest * 16, 16), 16), :].astype(
            BF16
        )


def wide_row(ref, row, size):
    return jnp.broadcast_to(ref[pl.ds(row, 1), :], (size, 128))


def sections_kernel(
    in_ref, out_ref, runs, codes, weights, residual, books_in, books_out, table, total
):
    @pl.loop(0, BLOCKS)
    def _(block):
        at = pl.ds(pl.multiple_of(block * 8, 8), 8)
        values = in_ref[block, 0:16, :].astype(F32)
        residual[0, at, :] = values[0:8]
        residual[1, at, :] = values[8:16]
        shared = in_ref[block, 16:48, :].astype(F32)
        weights[at, :] = shared[24:32]
        coded = shared[0:24]
        run = jnp.zeros_like(coded)
        for bit in range(5, -1, -1):
            over = coded >= 128.0 * 2.0 ** (1 << bit)
            coded = jnp.where(over, coded * 2.0 ** -(1 << bit), coded)
            run = run + jnp.where(over, float(1 << bit), 0.0)
        for section in range(SECTIONS):
            runs[section, at, :] = run[section * 8 : section * 8 + 8]
            codes[section, at, :] = coded[section * 8 : section * 8 + 8] - 128.0
        books_in[pl.ds(pl.multiple_of(block * 16, 16), 16), :] = in_ref[block, 48:64, :].astype(F32)

    books_out[...] = jnp.zeros_like(books_out)
    down = lax.broadcasted_iota(jnp.int32, (16, 128), 0).astype(F32)
    iotas = [(down + 16.0 * step).astype(BF16) for step in range(8)]
    nought = jnp.zeros((16, 128), BF16)
    one = jnp.ones((16, 128), BF16)

    def add_block(section, block):
        lefts, rights = [], []
        for row in range(8):
            at = block * 8 + row
            run = wide_row(runs.at[section], at, 16).astype(BF16)
            code = wide_row(codes.at[section], at, 16).astype(BF16)
            weight = wide_row(weights, at, 16).astype(BF16)
            first = wide_row(residual.at[0], at, 16).astype(BF16)
            second = wide_row(residual.at[1], at, 16).astype(BF16)
            masks = [run == iotas[step] for step in range(4)]
            lefts.append(
                jnp.concatenate(
                    [
                        jnp.where(mask, value, nought)
                        for value in (first, second, one)
                        for mask in masks
                    ],
                    axis=0,
                )
            )
            rights.append(
                jnp.concatenate(
                    [jnp.where(code == iotas[step], weight, nought) for step in range(8)], axis=0
                )
            )
        total[...] += lax.dot_general(
            jnp.concatenate(lefts, axis=1),
            jnp.concatenate(rights, axis=1),
            (((1,), (1,)), ((), ())),
            preferred_element_type=F32,
        )

    def take_block(section, block):
        at = pl.ds(pl.multiple_of(block * 8, 8), 8)
        run = runs[section, at, :]
        code = codes[section, at, :].astype(jnp.int32)
        rows = [jnp.zeros((8, 128), F32)] * 2
        for each in range(RUNS):
            mask = run == float(each)
            for which in range(2):
                wide = wide_row(table.at[which], each, 8)
                found = jnp.take_along_axis(wide, code, axis=1)
                rows[which] = jnp.where(mask, found, rows[which])
        result = []
        for which in range(2):
            left = (residual[which, at, :] - rows[which]).astype(BF16)
            residual[which, at, :] = left.astype(F32)
            result.append(left)
        return result

    def update(section):
        count = prior_weight + total[128:192, :]
        for which in range(2):
            book = jnp.concatenate(
                [
                    books_in[pl.ds(first * 16 + section * 2 + which, 8, stride=16), :]
                    + books_in[pl.ds(first * 16 + 8 + section * 2 + which, 8, stride=16), :]
                    for first in range(0, RUNS, 8)
                ],
                axis=0,
            )
            new = (prior_weight * book + total[which * 64 : which * 64 + 64, :]) / count
            table[which] = new
            parts = two_parts(new)
            for part in range(2):
                for first in range(0, RUNS, 8):
                    books_out[
                        pl.ds(first * 16 + part * 8 + section * 2 + which, 8, stride=16), :
                    ] = parts[part][first : first + 8]
        total[...] = jnp.zeros_like(total)

    total[...] = jnp.zeros_like(total)

    @pl.loop(0, BLOCKS)
    def _(block):
        add_block(0, block)

    update(0)
    for section in range(1, SECTIONS):

        @pl.loop(0, BLOCKS)
        def _(block):
            take_block(section - 1, block)
            add_block(section, block)

        update(section)

    @pl.loop(0, BLOCKS)
    def _(block):
        left = take_block(SECTIONS - 1, block)
        out_ref[block, 0:16, :] = jnp.concatenate(left, axis=0)
        out_ref[block, 16:32, :] = books_out[
            pl.ds(pl.multiple_of(block * 16, 16), 16), :
        ].astype(BF16)


def unpack_kernel(in_ref, book_ref, left_ref, error_ref, left_rows, book_rows):
    def one(source, error):
        rows = in_ref[source, 0:16, :].astype(F32)
        at = pl.ds(pl.multiple_of(source * 16, 16), 16)
        left_rows[at, :] = rows
        book_rows[at, :] = in_ref[source, 16:32, :].astype(F32)
        return error + rows[0:8] * rows[0:8] + rows[8:16] * rows[8:16]

    error_ref[...] = lax.fori_loop(0, RUNS, one, jnp.zeros((8, 128), F32))
    for block in range(8):
        turned = jnp.concatenate(
            [
                left_rows[pl.ds(first * 16 + which * 8 + block, 8, stride=16), :]
                for which in range(2)
                for first in range(0, RUNS, 8)
            ],
            axis=0,
        )
        left_ref[block * 128 : (block + 1) * 128, :] = turned.T.astype(BF16)
    for section in range(SECTIONS):
        turned = jnp.concatenate(
            [
                book_rows[pl.ds(first * 16 + section * 2 + which, 8, stride=16), :]
                + book_rows[pl.ds(first * 16 + 8 + section * 2 + which, 8, stride=16), :]
                for which in range(2)
                for first in range(0, RUNS, 8)
            ],
            axis=0,
        )
        book_ref[section] = turned.T


def per_device(embeddings, code_ids, codebooks, item_weight):
    params = pltpu.CompilerParams(vmem_limit_bytes=48 * 1024 * 1024)
    with jax.named_scope("pack"):
        packed = pl.pallas_call(
            pack_kernel,
            out_shape=jax.ShapeDtypeStruct((RUNS, ROWS_IN, 128), BF16),
            scratch_shapes=[
                pltpu.VMEM((RUNS * 16, 128), F32),
                pltpu.VMEM((RUNS * 16, 128), F32),
            ],
            compiler_params=params,
        )(embeddings, code_ids.reshape(24, 128), item_weight.reshape(8, 128), codebooks)
    with jax.named_scope("to_features"):
        mine = lax.all_to_all(packed, "dp", 0, 0, tiled=True)
    with jax.named_scope("sections"):
        done = pl.pallas_call(
            sections_kernel,
            out_shape=jax.ShapeDtypeStruct((BLOCKS, ROWS_OUT, 128), BF16),
            scratch_shapes=[
                pltpu.VMEM((SECTIONS, BLOCKS * 8, 128), F32),
                pltpu.VMEM((SECTIONS, BLOCKS * 8, 128), F32),
                pltpu.VMEM((BLOCKS * 8, 128), F32),
                pltpu.VMEM((2, BLOCKS * 8, 128), F32),
                pltpu.VMEM((RUNS * 16, 128), F32),
                pltpu.VMEM((RUNS * 16, 128), F32),
                pltpu.VMEM((2, RUNS, 128), F32),
                pltpu.VMEM((3 * RUNS, 128), F32),
            ],
            compiler_params=params,
        )(mine)
    with jax.named_scope("to_items"):
        back = lax.all_to_all(done, "dp", 0, 0, tiled=True)
    with jax.named_scope("unpack"):
        updated, left, error = pl.pallas_call(
            unpack_kernel,
            out_shape=(
                jax.ShapeDtypeStruct((SECTIONS, 128, FEATS), F32),
                jax.ShapeDtypeStruct((1024, FEATS), BF16),
                jax.ShapeDtypeStruct((8, 128), F32),
            ),
            scratch_shapes=[
                pltpu.VMEM((RUNS * 16, 128), F32),
                pltpu.VMEM((RUNS * 16, 128), F32),
            ],
            compiler_params=params,
        )(back)
    with jax.named_scope("error"):
        item_error = lax.psum(error, "feat").reshape(1024)
    return updated, left, item_error


def solution(mesh):
    in_specs = (P("dp", "feat"), P(None, "dp"), P(None, "dp", "feat"), P("dp"))
    out_specs = (P(None, "dp", "feat"), P("dp", "feat"), P("dp"))
    return jax.shard_map(
        per_device, mesh=mesh, in_specs=in_specs, out_specs=out_specs, check_vma=False
    )
```

```python
import jax
import jax.numpy as jnp
from jax import lax
from jax.experimental import pallas as pl
from jax.experimental.pallas import tpu as pltpu
from jax.sharding import PartitionSpec as P

F32 = jnp.float32
BF16 = jnp.bfloat16
SECTIONS = 3
RUNS = 64
BLOCKS = 64
FEATS = 128
prior_weight = 4.0
GROUP = 4

ROWS_IN = 64
ROWS_OUT = 32


def two_parts(x):
    head = x.astype(BF16).astype(F32)
    return head, x - head


def pack_kernel(
    emb_hbm, ids_hbm, w_hbm, book_hbm, out_ref, emb_ref, ids_ref, w_ref, book_ref, emb_rows, book_rows,
    shared_rows, sems
):
    pairs = ((ids_hbm, ids_ref), (w_hbm, w_ref), (emb_hbm, emb_ref), (book_hbm, book_ref))
    copies = [
        pltpu.make_async_copy(source, target, sems.at[at])
        for at, (source, target) in enumerate(pairs)
    ]
    for copy in copies:
        copy.start()
    book_rows[...] = jnp.zeros_like(book_rows)
    copies[0].wait()
    ids = ids_ref[...]
    run = ids >> 7
    coded = ((ids & 127) + 128).astype(F32)
    for bit in range(6):
        coded = coded * jnp.where((run >> bit) & 1 == 1, 2.0 ** (1 << bit), 1.0)
    for block in range(8):
        shared_rows[pl.ds(block, SECTIONS, stride=8), :] = coded[:, block * 128 : block * 128 + 128]
    copies[1].wait()
    shared_rows[24:32, :] = w_ref[...].astype(F32)
    shared = shared_rows[...].astype(BF16)
    copies[2].wait()
    for block in range(8):
        turned = emb_ref[block * 128 : (block + 1) * 128, :].astype(F32).T
        for group in range(16):
            which, first = group // 8, (group % 8) * 8
            emb_rows[pl.ds(first * 16 + which * 8 + block, 8, stride=16), :] = turned[
                group * 8 : (group + 1) * 8
            ]
    copies[3].wait()
    for section in range(SECTIONS):
        parts = two_parts(book_ref[section].T)
        for part in range(2):
            for group in range(16):
                which, first = group // 8, (group % 8) * 8
                book_rows[
                    pl.ds(first * 16 + part * 8 + section * 2 + which, 8, stride=16), :
                ] = parts[part][group * 8 : (group + 1) * 8]

    @pl.loop(0, RUNS)
    def _(dest):
        at = pl.ds(pl.multiple_of(dest * 16, 16), 16)
        out_ref[dest, 0:16, :] = emb_rows[at, :].astype(BF16)
        out_ref[dest, 16:48, :] = shared
        out_ref[dest, 48:64, :] = book_rows[at, :].astype(BF16)


def wide_row(ref, row, size):
    return jnp.broadcast_to(ref[pl.ds(row, 1), :], (size, 128))


def sections_kernel(
    in_ref, out_ref, runs, codes, weights, residual, books_in, books_out, table, total, fresh, stage
):
    @pl.loop(0, BLOCKS)
    def _(block):
        at = pl.ds(pl.multiple_of(block * 8, 8), 8)
        values = in_ref[block, 0:16, :].astype(F32)
        residual[0, at, :] = values[0:8]
        residual[1, at, :] = values[8:16]
        shared = in_ref[block, 16:48, :].astype(F32)
        weights[at, :] = shared[24:32]
        coded = shared[0:24]
        run = jnp.zeros_like(coded)
        for bit in range(5, -1, -1):
            over = coded >= 128.0 * 2.0 ** (1 << bit)
            coded = jnp.where(over, coded * 2.0 ** -(1 << bit), coded)
            run = run + jnp.where(over, float(1 << bit), 0.0)
        for section in range(SECTIONS):
            runs[section, at, :] = run[section * 8 : section * 8 + 8]
            codes[section, at, :] = coded[section * 8 : section * 8 + 8] - 128.0
        books_in[pl.ds(pl.multiple_of(block * 16, 16), 16), :] = in_ref[block, 48:64, :].astype(F32)

    books_out[...] = jnp.zeros_like(books_out)
    down = lax.broadcasted_iota(jnp.int32, (16, 128), 0).astype(F32)
    iotas = [(down + 16.0 * step).astype(BF16) for step in range(8)]
    nought = jnp.zeros((16, 128), BF16)
    one = jnp.ones((16, 128), BF16)

    def add_items(section, item_row, source, source_row, count):
        lefts, rights = [], []
        for row in range(count):
            at, source_at = item_row + row, source_row + row
            run = wide_row(runs.at[section], at, 16).astype(BF16)
            code = wide_row(codes.at[section], at, 16).astype(BF16)
            weight = wide_row(weights, at, 16).astype(BF16)
            first = wide_row(source.at[0], source_at, 16).astype(BF16)
            second = wide_row(source.at[1], source_at, 16).astype(BF16)
            masks = [run == iotas[step] for step in range(4)]
            lefts.append(
                jnp.concatenate(
                    [
                        jnp.where(mask, value, nought)
                        for value in (first, second, one)
                        for mask in masks
                    ],
                    axis=0,
                )
            )
            rights.append(
                jnp.concatenate(
                    [jnp.where(code == iotas[step], weight, nought) for step in range(8)], axis=0
                )
            )
        total[...] += lax.dot_general(
            jnp.concatenate(lefts, axis=1),
            jnp.concatenate(rights, axis=1),
            (((1,), (1,)), ((), ())),
            preferred_element_type=F32,
        )

    def take_block(section, block):
        at = pl.ds(pl.multiple_of(block * 8, 8), 8)
        run = runs[section, at, :]
        code = codes[section, at, :].astype(jnp.int32)
        rows = [jnp.zeros((8, 128), F32)] * 2
        for each in range(RUNS):
            mask = run == float(each)
            for which in range(2):
                wide = wide_row(table.at[which], each, 8)
                found = jnp.take_along_axis(wide, code, axis=1, mode='promise_in_bounds')
                rows[which] = jnp.where(mask, found, rows[which])
        result = []
        for which in range(2):
            left = (residual[which, at, :] - rows[which]).astype(BF16)
            residual[which, at, :] = left.astype(F32)
            result.append(left)
        return result

    def update(section):
        count = prior_weight + total[128:192, :]
        for which in range(2):
            book = jnp.concatenate(
                [
                    books_in[pl.ds(first * 16 + section * 2 + which, 8, stride=16), :]
                    + books_in[pl.ds(first * 16 + 8 + section * 2 + which, 8, stride=16), :]
                    for first in range(0, RUNS, 8)
                ],
                axis=0,
            )
            new = (prior_weight * book + total[which * 64 : which * 64 + 64, :]) / count
            table[which] = new
            parts = two_parts(new)
            for part in range(2):
                for first in range(0, RUNS, 8):
                    books_out[
                        pl.ds(first * 16 + part * 8 + section * 2 + which, 8, stride=16), :
                    ] = parts[part][first : first + 8]
        total[...] = jnp.zeros_like(total)

    total[...] = jnp.zeros_like(total)

    @pl.loop(0, BLOCKS // 8, unroll=2)
    def _(group):
        add_items(0, group * 64, residual, group * 64, 64)

    update(0)
    for section in range(1, SECTIONS):

        def take(group, step):
            left = take_block(section - 1, group * GROUP + step)
            for which in range(2):
                fresh[which, 8 * step : 8 * step + 8, :] = left[which].astype(F32)

        for step in range(GROUP):
            take(0, step)

        @pl.loop(1, BLOCKS // GROUP)
        def _(group):
            stage[...] = fresh[...]
            for step in range(GROUP):
                take(group, step)
                add_items(section, ((group - 1) * GROUP + step) * 8, stage, 8 * step, 8)

        add_items(section, (BLOCKS - GROUP) * 8, fresh, 0, 8 * GROUP)
        update(section)

    @pl.loop(0, BLOCKS, unroll=8)
    def _(block):
        left = take_block(SECTIONS - 1, block)
        out_ref[block, 0:16, :] = jnp.concatenate(left, axis=0)
        out_ref[block, 16:32, :] = books_out[
            pl.ds(pl.multiple_of(block * 16, 16), 16), :
        ].astype(BF16)


def error_kernel(in_ref, error_ref):
    def add(source, error):
        rows = in_ref[source, 0:16, :].astype(F32)
        return error + rows[0:8] * rows[0:8] + rows[8:16] * rows[8:16]

    error_ref[...] = lax.fori_loop(0, RUNS, add, jnp.zeros((8, 128), F32), unroll=8)


def unpack_kernel(in_ref, book_ref, left_ref, left_rows, book_rows):
    @pl.loop(0, RUNS, unroll=8)
    def _(source):
        at = pl.ds(pl.multiple_of(source * 16, 16), 16)
        left_rows[at, :] = in_ref[source, 0:16, :].astype(F32)
        book_rows[at, :] = in_ref[source, 16:32, :].astype(F32)

    for block in range(8):
        turned = jnp.concatenate(
            [
                left_rows[pl.ds(first * 16 + which * 8 + block, 8, stride=16), :]
                for which in range(2)
                for first in range(0, RUNS, 8)
            ],
            axis=0,
        )
        left_ref[block * 128 : (block + 1) * 128, :] = turned.T.astype(BF16)
    for section in range(SECTIONS):
        turned = jnp.concatenate(
            [
                book_rows[pl.ds(first * 16 + section * 2 + which, 8, stride=16), :]
                + book_rows[pl.ds(first * 16 + 8 + section * 2 + which, 8, stride=16), :]
                for which in range(2)
                for first in range(0, RUNS, 8)
            ],
            axis=0,
        )
        book_ref[section] = turned.T


def sum_over_feat(value):
    one, two, three = [
        lax.ppermute(value, "feat", [(at, (at + step) % 4) for at in range(4)])
        for step in range(1, 4)
    ]
    return (value + two) + (one + three)


def per_device(embeddings, code_ids, codebooks, item_weight):
    params = pltpu.CompilerParams(vmem_limit_bytes=48 * 1024 * 1024)
    with jax.named_scope("pack"):
        packed = pl.pallas_call(
            pack_kernel,
            out_shape=jax.ShapeDtypeStruct((RUNS, ROWS_IN, 128), BF16),
            in_specs=[pl.BlockSpec(memory_space=pltpu.HBM)] * 4,
            scratch_shapes=[
                pltpu.VMEM((1024, FEATS), BF16),
                pltpu.VMEM((SECTIONS, 1024), jnp.int32),
                pltpu.VMEM((8, 128), BF16),
                pltpu.VMEM((SECTIONS, 128, FEATS), F32),
                pltpu.VMEM((RUNS * 16, 128), F32),
                pltpu.VMEM((RUNS * 16, 128), F32),
                pltpu.VMEM((32, 128), F32),
                pltpu.SemaphoreType.DMA((4,)),
            ],
            compiler_params=pltpu.CompilerParams(vmem_limit_bytes=63 * 1024 * 1024),
        )(embeddings, code_ids, item_weight.reshape(8, 128), codebooks)
    with jax.named_scope("to_features"):
        mine = lax.all_to_all(packed, "dp", 0, 0, tiled=True)
    with jax.named_scope("sections"):
        done = pl.pallas_call(
            sections_kernel,
            out_shape=jax.ShapeDtypeStruct((BLOCKS, ROWS_OUT, 128), BF16),
            scratch_shapes=[
                pltpu.VMEM((SECTIONS, BLOCKS * 8, 128), F32),
                pltpu.VMEM((SECTIONS, BLOCKS * 8, 128), F32),
                pltpu.VMEM((BLOCKS * 8, 128), F32),
                pltpu.VMEM((2, BLOCKS * 8, 128), F32),
                pltpu.VMEM((RUNS * 16, 128), F32),
                pltpu.VMEM((RUNS * 16, 128), F32),
                pltpu.VMEM((2, RUNS, 128), F32),
                pltpu.VMEM((3 * RUNS, 128), F32),
                pltpu.VMEM((2, 8 * GROUP, 128), F32),
                pltpu.VMEM((2, 8 * GROUP, 128), F32),
            ],
            compiler_params=params,
        )(mine)
    with jax.named_scope("to_items"):
        back = lax.all_to_all(done, "dp", 0, 0, tiled=True)
    with jax.named_scope("error"):
        error = pl.pallas_call(
            error_kernel, out_shape=jax.ShapeDtypeStruct((8, 128), F32), compiler_params=params
        )(back)
        item_error = sum_over_feat(error).reshape(1024)
    with jax.named_scope("unpack"):
        updated, left = pl.pallas_call(
            unpack_kernel,
            out_shape=(
                jax.ShapeDtypeStruct((SECTIONS, 128, FEATS), F32),
                jax.ShapeDtypeStruct((1024, FEATS), BF16),
            ),
            scratch_shapes=[
                pltpu.VMEM((RUNS * 16, 128), F32),
                pltpu.VMEM((RUNS * 16, 128), F32),
            ],
            compiler_params=params,
        )(back)
    return updated, left, item_error


def solution(mesh):
    in_specs = (P("dp", "feat"), P(None, "dp"), P(None, "dp", "feat"), P("dp"))
    out_specs = (P(None, "dp", "feat"), P("dp", "feat"), P("dp"))
    return jax.shard_map(
        per_device, mesh=mesh, in_specs=in_specs, out_specs=out_specs, check_vma=False
    )
```

```python
import jax
import jax.numpy as jnp
from jax import lax
from jax.experimental import pallas as pl
from jax.experimental.pallas import tpu as pltpu
from jax.sharding import PartitionSpec as P

F32 = jnp.float32
BF16 = jnp.bfloat16
SECTIONS = 3
RUNS = 64
BLOCKS = 64
FEATS = 128
prior_weight = 4.0
GROUP = 8

ROWS_IN = 48
ROWS_OUT = 32


def two_parts(x):
    head = x.astype(BF16).astype(F32)
    return head, x - head


def pack_kernel(
    emb_hbm, ids_hbm, w_hbm, book_hbm, out_ref, emb_ref, ids_ref, w_ref, book_ref, emb_rows, book_rows,
    shared_rows, sems
):
    pairs = ((ids_hbm, ids_ref), (w_hbm, w_ref), (emb_hbm, emb_ref), (book_hbm, book_ref))
    copies = [
        pltpu.make_async_copy(source, target, sems.at[at])
        for at, (source, target) in enumerate(pairs)
    ]
    for copy in copies:
        copy.start()
    book_rows[...] = jnp.zeros_like(book_rows)
    copies[0].wait()
    ids = ids_ref[...]
    run = ids >> 7
    coded = ((ids & 127) + 128).astype(F32)
    for bit in range(6):
        coded = coded * jnp.where((run >> bit) & 1 == 1, 2.0 ** (1 << bit), 1.0)
    for block in range(8):
        shared_rows[pl.ds(block, SECTIONS, stride=8), :] = coded[:, block * 128 : block * 128 + 128]
    copies[1].wait()
    shared_rows[24:32, :] = w_ref[...].astype(F32)
    shared = shared_rows[...].astype(BF16)
    copies[2].wait()
    for block in range(8):
        turned = emb_ref[block * 128 : (block + 1) * 128, :].astype(F32).T
        for group in range(16):
            which, first = group // 8, (group % 8) * 8
            emb_rows[pl.ds(first * 16 + which * 8 + block, 8, stride=16), :] = turned[
                group * 8 : (group + 1) * 8
            ]
    copies[3].wait()
    for section in range(SECTIONS):
        parts = two_parts(book_ref[section].T)
        for part in range(2):
            for group in range(16):
                which, first = group // 8, (group % 8) * 8
                book_rows[
                    pl.ds(first * 16 + part * 8 + section * 2 + which, 8, stride=16), :
                ] = parts[part][group * 8 : (group + 1) * 8]

    @pl.loop(0, RUNS // 2, unroll=4)
    def _(chip):
        for core in range(2):
            dest = chip * 2 + core
            at = pl.ds(pl.multiple_of(dest * 16, 16), 16)
            out_ref[dest, 0:16, :] = emb_rows[at, :].astype(BF16)
            out_ref[dest, 16:32, :] = shared[core * 16 : core * 16 + 16]
            out_ref[dest, 32:48, :] = book_rows[at, :].astype(BF16)


def wide_row(ref, row, size):
    return jnp.broadcast_to(ref[pl.ds(row, 1), :], (size, 128))


def sections_kernel(
    in_ref, other_ref, out_ref, runs, codes, weights, residual, books_in, books_out, table, total, fresh, stage, steps
):
    is_first = lax.axis_index("dp") % 2 == 0

    @pl.loop(0, BLOCKS, unroll=2)
    def _(block):
        at = pl.ds(pl.multiple_of(block * 8, 8), 8)
        values = in_ref[block, 0:16, :].astype(F32)
        residual[0, at, :] = values[0:8]
        residual[1, at, :] = values[8:16]
        own = in_ref[block, 16:32, :].astype(F32)
        other = other_ref[block, 16:32, :].astype(F32)
        first = jnp.where(is_first, own, other)
        second = jnp.where(is_first, other, own)
        weights[at, :] = second[8:16]
        coded = jnp.concatenate([first, second[0:8]], axis=0)
        run = jnp.zeros_like(coded)
        for bit in range(5, -1, -1):
            over = coded >= 128.0 * 2.0 ** (1 << bit)
            coded = jnp.where(over, coded * 2.0 ** -(1 << bit), coded)
            run = run + jnp.where(over, float(1 << bit), 0.0)
        for section in range(SECTIONS):
            runs[section, at, :] = run[section * 8 : section * 8 + 8]
            codes[section, at, :] = coded[section * 8 : section * 8 + 8] - 128.0
        books_in[pl.ds(pl.multiple_of(block * 16, 16), 16), :] = in_ref[block, 32:48, :].astype(F32)

    books_out[...] = jnp.zeros_like(books_out)
    down = lax.broadcasted_iota(jnp.int32, (16, 128), 0).astype(F32)
    iotas = [(down + 16.0 * step).astype(BF16) for step in range(8)]
    nought = jnp.zeros((16, 128), BF16)
    one = jnp.ones((16, 128), BF16)

    def add_items(section, item_row, source, source_row, count):
        lefts, rights = [], []
        for row in range(count):
            at, source_at = item_row + row, source_row + row
            run = wide_row(runs.at[section], at, 16).astype(BF16)
            code = wide_row(codes.at[section], at, 16).astype(BF16)
            weight = wide_row(weights, at, 16).astype(BF16)
            first = wide_row(source.at[0], source_at, 16).astype(BF16)
            second = wide_row(source.at[1], source_at, 16).astype(BF16)
            masks = [run == iotas[step] for step in range(4)]
            lefts.append(
                jnp.concatenate(
                    [
                        jnp.where(mask, value, nought)
                        for value in (first, second, one)
                        for mask in masks
                    ],
                    axis=0,
                )
            )
            rights.append(
                jnp.concatenate(
                    [jnp.where(code == iotas[step], weight, nought) for step in range(8)], axis=0
                )
            )
        total[...] += lax.dot_general(
            jnp.concatenate(lefts, axis=1),
            jnp.concatenate(rights, axis=1),
            (((1,), (1,)), ((), ())),
            preferred_element_type=F32,
        )

    def take_block(section, block):
        at = pl.ds(pl.multiple_of(block * 8, 8), 8)
        run = runs[section, at, :]
        code = codes[section, at, :].astype(jnp.int32)
        both = jnp.zeros((8, 128), jnp.int32)
        for each in range(RUNS):
            found = jnp.take_along_axis(
                wide_row(table, each, 8), code, axis=1, mode="promise_in_bounds"
            )
            both = jnp.where(run == float(each), found, both)
        low = (both << 16) >> 16
        result = []
        for which, whole in enumerate(((both - low) >> 16, low)):
            row = whole.astype(F32) * steps[which : which + 1, :]
            left = (residual[which, at, :] - row).astype(BF16)
            residual[which, at, :] = left.astype(F32)
            result.append(left)
        return result

    def update(section):
        weight = total[128:192, :]
        count = prior_weight + weight
        levels = []
        for which in range(2):
            book = jnp.concatenate(
                [
                    books_in[pl.ds(first * 16 + section * 2 + which, 8, stride=16), :]
                    + books_in[pl.ds(first * 16 + 8 + section * 2 + which, 8, stride=16), :]
                    for first in range(0, RUNS, 8)
                ],
                axis=0,
            )
            new = (prior_weight * book + total[which * 64 : which * 64 + 64, :]) / count
            used = jnp.where(weight > 0.0, jnp.abs(new), 0.0)
            largest = jnp.max(jnp.max(used, axis=0, keepdims=True), axis=1, keepdims=True)
            step = jnp.maximum(largest, 1e-20) * (1.0 / 32767.0)
            steps[which : which + 1, :] = jnp.broadcast_to(step, (1, 128))
            level = jnp.clip(new / step, -32767.0, 32767.0)
            levels.append(jnp.round(level).astype(jnp.int32))
            parts = two_parts(new)
            for part in range(2):
                for first in range(0, RUNS, 8):
                    books_out[
                        pl.ds(first * 16 + part * 8 + section * 2 + which, 8, stride=16), :
                    ] = parts[part][first : first + 8]
        table[...] = levels[0] * 65536 + levels[1]
        total[...] = jnp.zeros_like(total)

    total[...] = jnp.zeros_like(total)

    @pl.loop(0, BLOCKS // 8, unroll=2)
    def _(group):
        add_items(0, group * 64, residual, group * 64, 64)

    update(0)
    for section in range(1, SECTIONS):

        def take(group, step):
            left = take_block(section - 1, group * GROUP + step)
            for which in range(2):
                fresh[which, 8 * step : 8 * step + 8, :] = left[which].astype(F32)

        for step in range(GROUP):
            take(0, step)

        @pl.loop(1, BLOCKS // GROUP)
        def _(group):
            stage[...] = fresh[...]
            for step in range(GROUP):
                take(group, step)
                add_items(section, ((group - 1) * GROUP + step) * 8, stage, 8 * step, 8)

        add_items(section, (BLOCKS - GROUP) * 8, fresh, 0, 8 * GROUP)
        update(section)

    @pl.loop(0, BLOCKS, unroll=8)
    def _(block):
        left = take_block(SECTIONS - 1, block)
        out_ref[block, 0:16, :] = jnp.concatenate(left, axis=0)
        out_ref[block, 16:32, :] = books_out[
            pl.ds(pl.multiple_of(block * 16, 16), 16), :
        ].astype(BF16)


def error_kernel(in_ref, error_ref):
    def add(source, error):
        rows = in_ref[source, 0:16, :].astype(F32)
        return error + rows[0:8] * rows[0:8] + rows[8:16] * rows[8:16]

    error_ref[...] = lax.fori_loop(0, RUNS, add, jnp.zeros((8, 128), F32), unroll=8)


def unpack_kernel(in_ref, book_ref, left_ref, left_rows, book_rows):
    @pl.loop(0, RUNS, unroll=8)
    def _(source):
        at = pl.ds(pl.multiple_of(source * 16, 16), 16)
        left_rows[at, :] = in_ref[source, 0:16, :].astype(F32)
        book_rows[at, :] = in_ref[source, 16:32, :].astype(F32)

    for block in range(8):
        turned = jnp.concatenate(
            [
                left_rows[pl.ds(first * 16 + which * 8 + block, 8, stride=16), :]
                for which in range(2)
                for first in range(0, RUNS, 8)
            ],
            axis=0,
        )
        left_ref[block * 128 : (block + 1) * 128, :] = turned.T.astype(BF16)
    for section in range(SECTIONS):
        turned = jnp.concatenate(
            [
                book_rows[pl.ds(first * 16 + section * 2 + which, 8, stride=16), :]
                + book_rows[pl.ds(first * 16 + 8 + section * 2 + which, 8, stride=16), :]
                for which in range(2)
                for first in range(0, RUNS, 8)
            ],
            axis=0,
        )
        book_ref[section] = turned.T


def sum_over_feat(value):
    one, two, three = [
        lax.ppermute(value, "feat", [(at, (at + step) % 4) for at in range(4)])
        for step in range(1, 4)
    ]
    return (value + two) + (one + three)


def per_device(embeddings, code_ids, codebooks, item_weight):
    params = pltpu.CompilerParams(vmem_limit_bytes=48 * 1024 * 1024)
    with jax.named_scope("pack"):
        packed = pl.pallas_call(
            pack_kernel,
            out_shape=jax.ShapeDtypeStruct((RUNS, ROWS_IN, 128), BF16),
            in_specs=[pl.BlockSpec(memory_space=pltpu.HBM)] * 4,
            scratch_shapes=[
                pltpu.VMEM((1024, FEATS), BF16),
                pltpu.VMEM((SECTIONS, 1024), jnp.int32),
                pltpu.VMEM((8, 128), BF16),
                pltpu.VMEM((SECTIONS, 128, FEATS), F32),
                pltpu.VMEM((RUNS * 16, 128), F32),
                pltpu.VMEM((RUNS * 16, 128), F32),
                pltpu.VMEM((32, 128), F32),
                pltpu.SemaphoreType.DMA((4,)),
            ],
            compiler_params=pltpu.CompilerParams(vmem_limit_bytes=63 * 1024 * 1024),
        )(embeddings, code_ids, item_weight.reshape(8, 128), codebooks)
    with jax.named_scope("to_features"):
        mine = lax.all_to_all(packed, "dp", 0, 0, tiled=True)
    with jax.named_scope("to_other_core"):
        other = lax.ppermute(mine, "dp", [(at, at ^ 1) for at in range(lax.axis_size("dp"))])
    with jax.named_scope("sections"):
        done = pl.pallas_call(
            sections_kernel,
            out_shape=jax.ShapeDtypeStruct((BLOCKS, ROWS_OUT, 128), BF16),
            scratch_shapes=[
                pltpu.VMEM((SECTIONS, BLOCKS * 8, 128), F32),
                pltpu.VMEM((SECTIONS, BLOCKS * 8, 128), F32),
                pltpu.VMEM((BLOCKS * 8, 128), F32),
                pltpu.VMEM((2, BLOCKS * 8, 128), F32),
                pltpu.VMEM((RUNS * 16, 128), F32),
                pltpu.VMEM((RUNS * 16, 128), F32),
                pltpu.VMEM((RUNS, 128), jnp.int32),
                pltpu.VMEM((3 * RUNS, 128), F32),
                pltpu.VMEM((2, 8 * GROUP, 128), F32),
                pltpu.VMEM((2, 8 * GROUP, 128), F32),
                pltpu.VMEM((8, 128), F32),
            ],
            compiler_params=params,
        )(mine, other)
    with jax.named_scope("to_items"):
        back = lax.all_to_all(done, "dp", 0, 0, tiled=True)
    with jax.named_scope("error"):
        error = pl.pallas_call(
            error_kernel, out_shape=jax.ShapeDtypeStruct((8, 128), F32), compiler_params=params
        )(back)
        item_error = sum_over_feat(error).reshape(1024)
    with jax.named_scope("unpack"):
        updated, left = pl.pallas_call(
            unpack_kernel,
            out_shape=(
                jax.ShapeDtypeStruct((SECTIONS, 128, FEATS), F32),
                jax.ShapeDtypeStruct((1024, FEATS), BF16),
            ),
            scratch_shapes=[
                pltpu.VMEM((RUNS * 16, 128), F32),
                pltpu.VMEM((RUNS * 16, 128), F32),
            ],
            compiler_params=params,
        )(back)
    return updated, left, item_error


def solution(mesh):
    in_specs = (P("dp", "feat"), P(None, "dp"), P(None, "dp", "feat"), P("dp"))
    out_specs = (P(None, "dp", "feat"), P("dp", "feat"), P("dp"))
    return jax.shard_map(
        per_device, mesh=mesh, in_specs=in_specs, out_specs=out_specs, check_vma=False
    )
```

```python
import jax
import jax.numpy as jnp
from jax import lax
from jax.experimental import pallas as pl
from jax.experimental.pallas import tpu as pltpu
from jax.sharding import PartitionSpec as P

F32 = jnp.float32
BF16 = jnp.bfloat16
SECTIONS = 3
RUNS = 64
BLOCKS = 64
FEATS = 128
prior_weight = 4.0
GROUP = 8

ROWS_IN = 48
ROWS_OUT = 24


def two_parts(x):
    head = x.astype(BF16).astype(F32)
    return head, x - head


def pack_kernel(
    emb_hbm, ids_hbm, w_hbm, book_hbm, out_ref, emb_ref, ids_ref, w_ref, book_ref, emb_rows, book_rows,
    shared_rows, sems
):
    pairs = ((ids_hbm, ids_ref), (w_hbm, w_ref), (emb_hbm, emb_ref), (book_hbm, book_ref))
    copies = [
        pltpu.make_async_copy(source, target, sems.at[at])
        for at, (source, target) in enumerate(pairs)
    ]
    for copy in copies:
        copy.start()
    book_rows[...] = jnp.zeros_like(book_rows)
    copies[0].wait()
    ids = ids_ref[...]
    run = ids >> 7
    coded = ((ids & 127) + 128).astype(F32)
    for bit in range(6):
        coded = coded * jnp.where((run >> bit) & 1 == 1, 2.0 ** (1 << bit), 1.0)
    for block in range(8):
        shared_rows[pl.ds(block, SECTIONS, stride=8), :] = coded[:, block * 128 : block * 128 + 128]
    copies[1].wait()
    shared_rows[24:32, :] = w_ref[...].astype(F32)
    shared = shared_rows[...].astype(BF16)
    copies[2].wait()
    for block in range(8):
        turned = emb_ref[block * 128 : (block + 1) * 128, :].astype(F32).T
        for group in range(16):
            which, first = group // 8, (group % 8) * 8
            emb_rows[pl.ds(first * 16 + which * 8 + block, 8, stride=16), :] = turned[
                group * 8 : (group + 1) * 8
            ]
    copies[3].wait()
    for section in range(SECTIONS):
        parts = two_parts(book_ref[section].T)
        for part in range(2):
            for group in range(16):
                which, first = group // 8, (group % 8) * 8
                book_rows[
                    pl.ds(first * 16 + part * 8 + section * 2 + which, 8, stride=16), :
                ] = parts[part][group * 8 : (group + 1) * 8]

    @pl.loop(0, RUNS // 2, unroll=4)
    def _(chip):
        for core in range(2):
            dest = chip * 2 + core
            at = pl.ds(pl.multiple_of(dest * 16, 16), 16)
            out_ref[dest, 0:16, :] = emb_rows[at, :].astype(BF16)
            out_ref[dest, 16:32, :] = shared[core * 16 : core * 16 + 16]
            out_ref[dest, 32:48, :] = book_rows[at, :].astype(BF16)


def wide_row(ref, row, size):
    return jnp.broadcast_to(ref[pl.ds(row, 1), :], (size, 128))


def sections_kernel(
    in_ref, other_ref, out_ref, runs, codes, weights, residual, books_in, books_out, table, total, fresh, stage, steps
):
    is_first = lax.axis_index("dp") % 2 == 0

    @pl.loop(0, BLOCKS, unroll=2)
    def _(block):
        at = pl.ds(pl.multiple_of(block * 8, 8), 8)
        values = in_ref[block, 0:16, :].astype(F32)
        residual[0, at, :] = values[0:8]
        residual[1, at, :] = values[8:16]
        own = in_ref[block, 16:32, :].astype(F32)
        other = other_ref[block, 16:32, :].astype(F32)
        first = jnp.where(is_first, own, other)
        second = jnp.where(is_first, other, own)
        weights[at, :] = second[8:16]
        coded = jnp.concatenate([first, second[0:8]], axis=0)
        run = jnp.zeros_like(coded)
        for bit in range(5, -1, -1):
            over = coded >= 128.0 * 2.0 ** (1 << bit)
            coded = jnp.where(over, coded * 2.0 ** -(1 << bit), coded)
            run = run + jnp.where(over, float(1 << bit), 0.0)
        for section in range(SECTIONS):
            runs[section, at, :] = run[section * 8 : section * 8 + 8]
            codes[section, at, :] = coded[section * 8 : section * 8 + 8] - 128.0
        books_in[pl.ds(pl.multiple_of(block * 16, 16), 16), :] = in_ref[block, 32:48, :].astype(F32)

    books_out[...] = jnp.zeros_like(books_out)
    down = lax.broadcasted_iota(jnp.int32, (16, 128), 0).astype(F32)
    iotas = [(down + 16.0 * step).astype(BF16) for step in range(8)]
    nought = jnp.zeros((16, 128), BF16)
    one = jnp.ones((16, 128), BF16)

    def add_items(section, item_row, source, source_row, count):
        lefts, rights = [], []
        for row in range(count):
            at, source_at = item_row + row, source_row + row
            run = wide_row(runs.at[section], at, 16).astype(BF16)
            code = wide_row(codes.at[section], at, 16).astype(BF16)
            weight = wide_row(weights, at, 16).astype(BF16)
            first = wide_row(source.at[0], source_at, 16).astype(BF16)
            second = wide_row(source.at[1], source_at, 16).astype(BF16)
            masks = [run == iotas[step] for step in range(4)]
            lefts.append(
                jnp.concatenate(
                    [
                        jnp.where(mask, value, nought)
                        for value in (first, second, one)
                        for mask in masks
                    ],
                    axis=0,
                )
            )
            rights.append(
                jnp.concatenate(
                    [jnp.where(code == iotas[step], weight, nought) for step in range(8)], axis=0
                )
            )
        total[...] += lax.dot_general(
            jnp.concatenate(lefts, axis=1),
            jnp.concatenate(rights, axis=1),
            (((1,), (1,)), ((), ())),
            preferred_element_type=F32,
        )

    def take_block(section, block):
        at = pl.ds(pl.multiple_of(block * 8, 8), 8)
        run = runs[section, at, :]
        code = codes[section, at, :].astype(jnp.int32)
        both = jnp.zeros((8, 128), jnp.int32)
        for each in range(RUNS):
            found = jnp.take_along_axis(
                wide_row(table, each, 8), code, axis=1, mode="promise_in_bounds"
            )
            both = jnp.where(run == float(each), found, both)
        low = (both << 16) >> 16
        result = []
        for which, whole in enumerate(((both - low) >> 16, low)):
            row = whole.astype(F32) * steps[which : which + 1, :]
            left = (residual[which, at, :] - row).astype(BF16)
            residual[which, at, :] = left.astype(F32)
            result.append(left)
        return result

    def update(section):
        weight = total[128:192, :]
        count = prior_weight + weight
        levels = []
        for which in range(2):
            book = jnp.concatenate(
                [
                    books_in[pl.ds(first * 16 + section * 2 + which, 8, stride=16), :]
                    + books_in[pl.ds(first * 16 + 8 + section * 2 + which, 8, stride=16), :]
                    for first in range(0, RUNS, 8)
                ],
                axis=0,
            )
            new = (prior_weight * book + total[which * 64 : which * 64 + 64, :]) / count
            used = jnp.where(weight > 0.0, jnp.abs(new), 0.0)
            largest = jnp.max(jnp.max(used, axis=0, keepdims=True), axis=1, keepdims=True)
            step = jnp.maximum(largest, 1e-20) * (1.0 / 32767.0)
            steps[which : which + 1, :] = jnp.broadcast_to(step, (1, 128))
            level = jnp.clip(new / step, -32767.0, 32767.0)
            levels.append(jnp.round(level).astype(jnp.int32))
            for first in range(0, RUNS, 8):
                books_out[pl.ds(first * 8 + section * 2 + which, 8, stride=8), :] = new[
                    first : first + 8
                ]
        table[...] = levels[0] * 65536 + levels[1]
        total[...] = jnp.zeros_like(total)

    total[...] = jnp.zeros_like(total)

    @pl.loop(0, BLOCKS // 8, unroll=2)
    def _(group):
        add_items(0, group * 64, residual, group * 64, 64)

    update(0)
    for section in range(1, SECTIONS):

        def take(group, step):
            left = take_block(section - 1, group * GROUP + step)
            for which in range(2):
                fresh[which, 8 * step : 8 * step + 8, :] = left[which].astype(F32)

        for step in range(GROUP):
            take(0, step)

        @pl.loop(1, BLOCKS // GROUP)
        def _(group):
            stage[...] = fresh[...]
            for step in range(GROUP):
                take(group, step)
                add_items(section, ((group - 1) * GROUP + step) * 8, stage, 8 * step, 8)

        add_items(section, (BLOCKS - GROUP) * 8, fresh, 0, 8 * GROUP)
        update(section)

    @pl.loop(0, BLOCKS, unroll=8)
    def _(block):
        left = take_block(SECTIONS - 1, block)
        books = books_out[pl.ds(pl.multiple_of(block * 8, 8), 8), :]
        rows = [left[0].astype(F32), left[1].astype(F32), books]
        out_ref[block] = jnp.concatenate(rows, axis=0).astype(BF16)


def error_kernel(in_ref, error_ref):
    def add(source, error):
        rows = in_ref[source].astype(F32)
        return error + rows[0:8] * rows[0:8] + rows[8:16] * rows[8:16]

    error_ref[...] = lax.fori_loop(0, RUNS, add, jnp.zeros((8, 128), F32), unroll=8)


def unpack_kernel(in_ref, book_ref, left_ref, left_rows, book_rows):
    @pl.loop(0, RUNS, unroll=8)
    def _(source):
        rows = in_ref[source].astype(F32)
        left_rows[pl.ds(pl.multiple_of(source * 16, 16), 16), :] = rows[0:16]
        book_rows[pl.ds(pl.multiple_of(source * 8, 8), 8), :] = rows[16:24]

    for block in range(8):
        turned = jnp.concatenate(
            [
                left_rows[pl.ds(first * 16 + which * 8 + block, 8, stride=16), :]
                for which in range(2)
                for first in range(0, RUNS, 8)
            ],
            axis=0,
        )
        left_ref[block * 128 : (block + 1) * 128, :] = turned.T.astype(BF16)
    for section in range(SECTIONS):
        turned = jnp.concatenate(
            [
                book_rows[pl.ds(first * 8 + section * 2 + which, 8, stride=8), :]
                for which in range(2)
                for first in range(0, RUNS, 8)
            ],
            axis=0,
        )
        book_ref[section] = turned.T


def sum_over_feat(value):
    one, two, three = [
        lax.ppermute(value, "feat", [(at, (at + step) % 4) for at in range(4)])
        for step in range(1, 4)
    ]
    return (value + two) + (one + three)


def per_device(embeddings, code_ids, codebooks, item_weight):
    params = pltpu.CompilerParams(vmem_limit_bytes=48 * 1024 * 1024)
    with jax.named_scope("pack"):
        packed = pl.pallas_call(
            pack_kernel,
            out_shape=jax.ShapeDtypeStruct((RUNS, ROWS_IN, 128), BF16),
            in_specs=[pl.BlockSpec(memory_space=pltpu.HBM)] * 4,
            scratch_shapes=[
                pltpu.VMEM((1024, FEATS), BF16),
                pltpu.VMEM((SECTIONS, 1024), jnp.int32),
                pltpu.VMEM((8, 128), BF16),
                pltpu.VMEM((SECTIONS, 128, FEATS), F32),
                pltpu.VMEM((RUNS * 16, 128), F32),
                pltpu.VMEM((RUNS * 16, 128), F32),
                pltpu.VMEM((32, 128), F32),
                pltpu.SemaphoreType.DMA((4,)),
            ],
            compiler_params=pltpu.CompilerParams(vmem_limit_bytes=63 * 1024 * 1024),
        )(embeddings, code_ids, item_weight.reshape(8, 128), codebooks)
    with jax.named_scope("to_features"):
        mine = lax.all_to_all(packed, "dp", 0, 0, tiled=True)
    with jax.named_scope("to_other_core"):
        other = lax.ppermute(mine, "dp", [(at, at ^ 1) for at in range(lax.axis_size("dp"))])
    with jax.named_scope("sections"):
        done = pl.pallas_call(
            sections_kernel,
            out_shape=jax.ShapeDtypeStruct((BLOCKS, ROWS_OUT, 128), BF16),
            scratch_shapes=[
                pltpu.VMEM((SECTIONS, BLOCKS * 8, 128), F32),
                pltpu.VMEM((SECTIONS, BLOCKS * 8, 128), F32),
                pltpu.VMEM((BLOCKS * 8, 128), F32),
                pltpu.VMEM((2, BLOCKS * 8, 128), F32),
                pltpu.VMEM((RUNS * 16, 128), F32),
                pltpu.VMEM((RUNS * 8, 128), F32),
                pltpu.VMEM((RUNS, 128), jnp.int32),
                pltpu.VMEM((3 * RUNS, 128), F32),
                pltpu.VMEM((2, 8 * GROUP, 128), F32),
                pltpu.VMEM((2, 8 * GROUP, 128), F32),
                pltpu.VMEM((8, 128), F32),
            ],
            compiler_params=params,
        )(mine, other)
    with jax.named_scope("to_items"):
        back = lax.all_to_all(done, "dp", 0, 0, tiled=True)
    with jax.named_scope("error"):
        error = pl.pallas_call(
            error_kernel, out_shape=jax.ShapeDtypeStruct((8, 128), F32), compiler_params=params
        )(back)
        item_error = sum_over_feat(error).reshape(1024)
    with jax.named_scope("unpack"):
        updated, left = pl.pallas_call(
            unpack_kernel,
            out_shape=(
                jax.ShapeDtypeStruct((SECTIONS, 128, FEATS), F32),
                jax.ShapeDtypeStruct((1024, FEATS), BF16),
            ),
            scratch_shapes=[
                pltpu.VMEM((RUNS * 16, 128), F32),
                pltpu.VMEM((RUNS * 8, 128), F32),
            ],
            compiler_params=params,
        )(back)
    return updated, left, item_error


def solution(mesh):
    in_specs = (P("dp", "feat"), P(None, "dp"), P(None, "dp", "feat"), P("dp"))
    out_specs = (P(None, "dp", "feat"), P("dp", "feat"), P("dp"))
    return jax.shard_map(
        per_device, mesh=mesh, in_specs=in_specs, out_specs=out_specs, check_vma=False
    )
```

```python
import jax
import jax.numpy as jnp
from jax import lax
from jax.experimental import pallas as pl
from jax.experimental.pallas import tpu as pltpu
from jax.sharding import Mesh
from jax.sharding import PartitionSpec as P

F32 = jnp.float32
BF16 = jnp.bfloat16
SECTIONS = 3
RUNS = 64
BLOCKS = 64
FEATS = 128
prior_weight = 4.0
GROUP = 8

CHIPS = 32
ROWS_IN = 88
ROWS_OUT = 24


def two_parts(x):
    head = x.astype(BF16).astype(F32)
    return head, x - head


def pack_kernel(
    emb_hbm, ids_hbm, w_hbm, book_hbm, out_ref, emb_ref, ids_ref, w_ref, book_ref, emb_rows, book_rows,
    shared_rows, sems
):
    pairs = ((ids_hbm, ids_ref), (w_hbm, w_ref), (emb_hbm, emb_ref), (book_hbm, book_ref))
    copies = [
        pltpu.make_async_copy(source, target, sems.at[at])
        for at, (source, target) in enumerate(pairs)
    ]
    for copy in copies:
        copy.start()
    book_rows[...] = jnp.zeros_like(book_rows)
    copies[0].wait()
    ids = ids_ref[...]
    run = ids >> 7
    coded = ((ids & 127) + 128).astype(F32)
    for bit in range(6):
        coded = coded * jnp.where((run >> bit) & 1 == 1, 2.0 ** (1 << bit), 1.0)
    for block in range(8):
        shared_rows[pl.ds(block, SECTIONS, stride=8), :] = coded[:, block * 128 : block * 128 + 128]
    copies[1].wait()
    shared_rows[24:32, :] = w_ref[...].astype(F32)
    copies[2].wait()
    for block in range(8):
        turned = emb_ref[block * 128 : (block + 1) * 128, :].astype(F32).T
        for group in range(16):
            which, first = group // 8, (group % 8) * 8
            emb_rows[pl.ds(first * 16 + which * 8 + block, 8, stride=16), :] = turned[
                group * 8 : (group + 1) * 8
            ]
    copies[3].wait()
    for section in range(SECTIONS):
        parts = two_parts(book_ref[section].T)
        for part in range(2):
            for group in range(16):
                which, first = group // 8, (group % 8) * 8
                book_rows[
                    pl.ds(first * 16 + part * 6 + section * 2 + which, 8, stride=16), :
                ] = parts[part][group * 8 : (group + 1) * 8]

    shared = shared_rows[...]

    @pl.loop(0, CHIPS, unroll=4)
    def _(chip):
        at = pl.ds(pl.multiple_of(chip * 32, 32), 32)
        books = book_rows[at, :]
        rows = [emb_rows[at, :], shared, books[0:8], books[16:24], books[8:12], books[24:28]]
        out_ref[chip] = jnp.concatenate(rows, axis=0).astype(BF16)


def open_chip(rows, is_first):
    rows = rows.astype(F32)
    values = jnp.where(is_first, rows[0:16], rows[16:32])
    last = jnp.concatenate([rows[84:88], rows[80:84]], axis=0)
    books = [
        jnp.where(is_first, rows[64:72], rows[72:80]),
        jnp.where(is_first, rows[80:88], last),
    ]
    return values, rows[32:56], rows[56:64], jnp.concatenate(books, axis=0)


def run_and_code(coded):
    run = jnp.zeros_like(coded)
    for bit in range(5, -1, -1):
        over = coded >= 128.0 * 2.0 ** (1 << bit)
        coded = jnp.where(over, coded * 2.0 ** -(1 << bit), coded)
        run = run + jnp.where(over, float(1 << bit), 0.0)
    return run, coded - 128.0


def wide_row(ref, row, size):
    return jnp.broadcast_to(ref[pl.ds(row, 1), :], (size, 128))


def adder(runs, codes, weights, total):
    down = lax.broadcasted_iota(jnp.int32, (16, 128), 0).astype(F32)
    iotas = [(down + 16.0 * step).astype(BF16) for step in range(8)]
    nought = jnp.zeros((16, 128), BF16)
    one = jnp.ones((16, 128), BF16)

    def add_items(section, item_row, source, source_row, count):
        lefts, rights = [], []
        for row in range(count):
            at, source_at = item_row + row, source_row + row
            run = wide_row(runs.at[section], at, 16).astype(BF16)
            code = wide_row(codes.at[section], at, 16).astype(BF16)
            weight = wide_row(weights, at, 16).astype(BF16)
            first = wide_row(source.at[0], source_at, 16).astype(BF16)
            second = wide_row(source.at[1], source_at, 16).astype(BF16)
            masks = [run == iotas[step] for step in range(4)]
            lefts.append(
                jnp.concatenate(
                    [
                        jnp.where(mask, value, nought)
                        for value in (first, second, one)
                        for mask in masks
                    ],
                    axis=0,
                )
            )
            rights.append(
                jnp.concatenate(
                    [jnp.where(code == iotas[step], weight, nought) for step in range(8)], axis=0
                )
            )
        total[...] += lax.dot_general(
            jnp.concatenate(lefts, axis=1),
            jnp.concatenate(rights, axis=1),
            (((1,), (1,)), ((), ())),
            preferred_element_type=F32,
        )

    return add_items


def first_kernel(in_ref, total, runs, codes, weights, residual):
    is_first = lax.axis_index("core") == 0

    @pl.loop(0, CHIPS, unroll=2)
    def _(chip):
        at = pl.ds(pl.multiple_of(chip * 8, 8), 8)
        values, coded, weight, _ = open_chip(in_ref[chip], is_first)
        residual[0, at, :] = values[0:8]
        residual[1, at, :] = values[8:16]
        weights[at, :] = weight
        runs[0, at, :], codes[0, at, :] = run_and_code(coded[0:8])

    add_items = adder(runs, codes, weights, total)
    total[...] = jnp.zeros_like(total)

    @pl.loop(0, CHIPS // 8, unroll=2)
    def _(group):
        add_items(0, group * 64, residual, group * 64, 64)


def sections_kernel(
    in_ref, other_ref, first_ref, out_ref, runs, codes, weights, residual, books_in, books_out, table, total,
    fresh, stage, steps
):
    core = lax.axis_index("core")
    is_first = core == 0

    for half, ref in enumerate((in_ref, other_ref)):

        @pl.loop(0, CHIPS, unroll=2)
        def _(chip):
            at = pl.ds(pl.multiple_of((half * CHIPS + chip) * 8, 8), 8)
            values, coded, weight, books = open_chip(ref[chip], is_first)
            residual[0, at, :] = values[0:8]
            residual[1, at, :] = values[8:16]
            weights[at, :] = weight
            run, code = run_and_code(coded)
            for section in range(SECTIONS):
                runs[section, at, :] = run[section * 8 : section * 8 + 8]
                codes[section, at, :] = code[section * 8 : section * 8 + 8]
            source = chip * 2 + (core if half == 0 else 1 - core)
            books_in[pl.ds(pl.multiple_of(source * 16, 16), 16), :] = books

    books_out[...] = jnp.zeros_like(books_out)
    add_items = adder(runs, codes, weights, total)

    def take_block(section, block):
        at = pl.ds(pl.multiple_of(block * 8, 8), 8)
        run = runs[section, at, :]
        code = codes[section, at, :].astype(jnp.int32)
        both = jnp.zeros((8, 128), jnp.int32)
        for each in range(RUNS):
            found = jnp.take_along_axis(
                wide_row(table, each, 8), code, axis=1, mode="promise_in_bounds"
            )
            both = jnp.where(run == float(each), found, both)
        low = (both << 16) >> 16
        result = []
        for which, whole in enumerate(((both - low) >> 16, low)):
            row = whole.astype(F32) * steps[which : which + 1, :]
            left = (residual[which, at, :] - row).astype(BF16)
            residual[which, at, :] = left.astype(F32)
            result.append(left)
        return result

    def update(section):
        weight = total[128:192, :]
        count = prior_weight + weight
        levels = []
        for which in range(2):
            book = jnp.concatenate(
                [
                    books_in[pl.ds(first * 16 + section * 2 + which, 8, stride=16), :]
                    + books_in[pl.ds(first * 16 + 6 + section * 2 + which, 8, stride=16), :]
                    for first in range(0, RUNS, 8)
                ],
                axis=0,
            )
            new = (prior_weight * book + total[which * 64 : which * 64 + 64, :]) / count
            used = jnp.where(weight > 0.0, jnp.abs(new), 0.0)
            largest = jnp.max(jnp.max(used, axis=0, keepdims=True), axis=1, keepdims=True)
            step = jnp.maximum(largest, 1e-20) * (1.0 / 32767.0)
            steps[which : which + 1, :] = jnp.broadcast_to(step, (1, 128))
            level = jnp.clip(new / step, -32767.0, 32767.0)
            levels.append(jnp.round(level).astype(jnp.int32))
            for first in range(0, RUNS, 8):
                books_out[pl.ds(first * 8 + section * 2 + which, 8, stride=8), :] = new[
                    first : first + 8
                ]
        table[...] = levels[0] * 65536 + levels[1]
        total[...] = jnp.zeros_like(total)

    total[...] = first_ref[...]

    @pl.loop(CHIPS // 8, BLOCKS // 8, unroll=2)
    def _(group):
        add_items(0, group * 64, residual, group * 64, 64)

    update(0)
    for section in range(1, SECTIONS):

        def take(group, step):
            left = take_block(section - 1, group * GROUP + step)
            for which in range(2):
                fresh[which, 8 * step : 8 * step + 8, :] = left[which].astype(F32)

        for step in range(GROUP):
            take(0, step)

        @pl.loop(1, BLOCKS // GROUP)
        def _(group):
            stage[...] = fresh[...]
            for step in range(GROUP):
                take(group, step)
                add_items(section, ((group - 1) * GROUP + step) * 8, stage, 8 * step, 8)

        add_items(section, (BLOCKS - GROUP) * 8, fresh, 0, 8 * GROUP)
        update(section)

    for half in range(2):

        @pl.loop(0, CHIPS, unroll=8)
        def _(chip):
            left = take_block(SECTIONS - 1, half * CHIPS + chip)
            source = chip * 2 + (core if half == 0 else 1 - core)
            books = books_out[pl.ds(pl.multiple_of(source * 8, 8), 8), :]
            rows = [left[0].astype(F32), left[1].astype(F32), books]
            out_ref[source] = jnp.concatenate(rows, axis=0).astype(BF16)


def error_kernel(in_ref, error_ref):
    def add(source, error):
        rows = in_ref[source].astype(F32)
        return error + rows[0:8] * rows[0:8] + rows[8:16] * rows[8:16]

    error_ref[...] = lax.fori_loop(0, RUNS, add, jnp.zeros((8, 128), F32), unroll=8)


def unpack_kernel(in_ref, book_ref, left_ref, left_rows, book_rows):
    @pl.loop(0, RUNS, unroll=8)
    def _(source):
        rows = in_ref[source].astype(F32)
        left_rows[pl.ds(pl.multiple_of(source * 16, 16), 16), :] = rows[0:16]
        book_rows[pl.ds(pl.multiple_of(source * 8, 8), 8), :] = rows[16:24]

    for block in range(8):
        turned = jnp.concatenate(
            [
                left_rows[pl.ds(first * 16 + which * 8 + block, 8, stride=16), :]
                for which in range(2)
                for first in range(0, RUNS, 8)
            ],
            axis=0,
        )
        left_ref[block * 128 : (block + 1) * 128, :] = turned.T.astype(BF16)
    for section in range(SECTIONS):
        turned = jnp.concatenate(
            [
                book_rows[pl.ds(first * 8 + section * 2 + which, 8, stride=8), :]
                for which in range(2)
                for first in range(0, RUNS, 8)
            ],
            axis=0,
        )
        book_ref[section] = turned.T


def sum_over_feat(value):
    one, two, three = [
        lax.ppermute(value, "feat", [(at, (at + step) % 4) for at in range(4)])
        for step in range(1, 4)
    ]
    return (value + two) + (one + three)


def per_device(embeddings, code_ids, codebooks, item_weight):
    params = pltpu.CompilerParams(vmem_limit_bytes=48 * 1024 * 1024)
    with jax.named_scope("pack"):
        packed = pl.pallas_call(
            pack_kernel,
            out_shape=jax.ShapeDtypeStruct((CHIPS, ROWS_IN, 128), BF16),
            in_specs=[pl.BlockSpec(memory_space=pltpu.HBM)] * 4,
            scratch_shapes=[
                pltpu.VMEM((1024, FEATS), BF16),
                pltpu.VMEM((SECTIONS, 1024), jnp.int32),
                pltpu.VMEM((8, 128), BF16),
                pltpu.VMEM((SECTIONS, 128, FEATS), F32),
                pltpu.VMEM((RUNS * 16, 128), F32),
                pltpu.VMEM((RUNS * 16, 128), F32),
                pltpu.VMEM((32, 128), F32),
                pltpu.SemaphoreType.DMA((4,)),
            ],
            compiler_params=pltpu.CompilerParams(vmem_limit_bytes=63 * 1024 * 1024),
        )(embeddings, code_ids, item_weight.reshape(8, 128), codebooks)
    with jax.named_scope("to_features"):
        mine = lax.all_to_all(packed, "chip", 0, 0, tiled=True)
    with jax.named_scope("to_other_core"):
        other = lax.ppermute(mine, "core", [(0, 1), (1, 0)])
    with jax.named_scope("first_sums"):
        first = pl.pallas_call(
            first_kernel,
            out_shape=jax.ShapeDtypeStruct((3 * RUNS, 128), F32),
            scratch_shapes=[
                pltpu.VMEM((1, CHIPS * 8, 128), F32),
                pltpu.VMEM((1, CHIPS * 8, 128), F32),
                pltpu.VMEM((CHIPS * 8, 128), F32),
                pltpu.VMEM((2, CHIPS * 8, 128), F32),
            ],
            compiler_params=params,
            cost_estimate=pl.CostEstimate(
                flops=2 * 3 * RUNS * 128 * CHIPS * 1024, bytes_accessed=2**20, transcendentals=0
            ),
        )(mine)
    with jax.named_scope("sections"):
        done = pl.pallas_call(
            sections_kernel,
            out_shape=jax.ShapeDtypeStruct((BLOCKS, ROWS_OUT, 128), BF16),
            scratch_shapes=[
                pltpu.VMEM((SECTIONS, BLOCKS * 8, 128), F32),
                pltpu.VMEM((SECTIONS, BLOCKS * 8, 128), F32),
                pltpu.VMEM((BLOCKS * 8, 128), F32),
                pltpu.VMEM((2, BLOCKS * 8, 128), F32),
                pltpu.VMEM((RUNS * 16, 128), F32),
                pltpu.VMEM((RUNS * 8, 128), F32),
                pltpu.VMEM((RUNS, 128), jnp.int32),
                pltpu.VMEM((3 * RUNS, 128), F32),
                pltpu.VMEM((2, 8 * GROUP, 128), F32),
                pltpu.VMEM((2, 8 * GROUP, 128), F32),
                pltpu.VMEM((8, 128), F32),
            ],
            compiler_params=params,
        )(mine, other, first)
    with jax.named_scope("to_items"):
        back = lax.all_to_all(done, ("chip", "core"), 0, 0, tiled=True)
    with jax.named_scope("error"):
        error = pl.pallas_call(
            error_kernel, out_shape=jax.ShapeDtypeStruct((8, 128), F32), compiler_params=params
        )(back)
        item_error = sum_over_feat(error).reshape(1024)
    with jax.named_scope("unpack"):
        updated, left = pl.pallas_call(
            unpack_kernel,
            out_shape=(
                jax.ShapeDtypeStruct((SECTIONS, 128, FEATS), F32),
                jax.ShapeDtypeStruct((1024, FEATS), BF16),
            ),
            scratch_shapes=[
                pltpu.VMEM((RUNS * 16, 128), F32),
                pltpu.VMEM((RUNS * 8, 128), F32),
            ],
            compiler_params=params,
        )(back)
    return updated, left, item_error


def solution(mesh):
    dp, feat = mesh.devices.shape
    split = Mesh(mesh.devices.reshape(dp // 2, 2, feat), ("chip", "core", "feat"))
    dp_axes = ("chip", "core")
    in_specs = (P(dp_axes, "feat"), P(None, dp_axes), P(None, dp_axes, "feat"), P(dp_axes))
    out_specs = (P(None, dp_axes, "feat"), P(dp_axes, "feat"), P(dp_axes))
    return jax.shard_map(
        per_device, mesh=split, in_specs=in_specs, out_specs=out_specs, check_vma=False
    )
```

```python
import jax
import jax.numpy as jnp
from jax import lax
from jax.experimental import pallas as pl
from jax.experimental.pallas import tpu as pltpu
from jax.sharding import Mesh
from jax.sharding import PartitionSpec as P

F32 = jnp.float32
BF16 = jnp.bfloat16
SECTIONS = 3
RUNS = 64
BLOCKS = 64
FEATS = 128
prior_weight = 4.0
GROUP = 8

CHIPS = 32
Z_BITS = ("z2", "z1", "z0")
CHIP_PLACES = ("y", "z0", "z1", "z2")
DP = (*Z_BITS, "y", "core")
ROWS_IN = 88
ROWS_OUT = 24


def two_parts(x):
    head = x.astype(BF16).astype(F32)
    return head, x - head


def pack_kernel(
    emb_hbm, ids_hbm, w_hbm, book_hbm, out_ref, emb_ref, ids_ref, w_ref, book_ref, emb_rows, book_rows,
    shared_rows, sems
):
    pairs = ((ids_hbm, ids_ref), (w_hbm, w_ref), (emb_hbm, emb_ref), (book_hbm, book_ref))
    copies = [
        pltpu.make_async_copy(source, target, sems.at[at])
        for at, (source, target) in enumerate(pairs)
    ]
    for copy in copies:
        copy.start()
    book_rows[...] = jnp.zeros_like(book_rows)
    copies[0].wait()
    ids = ids_ref[...]
    run = ids >> 7
    coded = ((ids & 127) + 128).astype(F32)
    for bit in range(6):
        coded = coded * jnp.where((run >> bit) & 1 == 1, 2.0 ** (1 << bit), 1.0)
    for block in range(8):
        shared_rows[pl.ds(block, SECTIONS, stride=8), :] = coded[:, block * 128 : block * 128 + 128]
    copies[1].wait()
    shared_rows[24:32, :] = w_ref[...].astype(F32)
    copies[2].wait()
    for block in range(8):
        turned = emb_ref[block * 128 : (block + 1) * 128, :].astype(F32).T
        for group in range(16):
            which, first = group // 8, (group % 8) * 8
            emb_rows[pl.ds(first * 16 + which * 8 + block, 8, stride=16), :] = turned[
                group * 8 : (group + 1) * 8
            ]
    copies[3].wait()
    for section in range(SECTIONS):
        parts = two_parts(book_ref[section].T)
        for part in range(2):
            for group in range(16):
                which, first = group // 8, (group % 8) * 8
                book_rows[
                    pl.ds(first * 16 + part * 6 + section * 2 + which, 8, stride=16), :
                ] = parts[part][group * 8 : (group + 1) * 8]

    shared = shared_rows[...]

    @pl.loop(0, CHIPS, unroll=4)
    def _(chip):
        at = pl.ds(pl.multiple_of(chip * 32, 32), 32)
        books = book_rows[at, :]
        rows = [emb_rows[at, :], shared, books[0:8], books[16:24], books[8:12], books[24:28]]
        out_ref[place_of(chip)] = jnp.concatenate(rows, axis=0).astype(BF16)


def place_of(chip):
    return (chip & 3) * 8 + ((chip >> 2) & 1) * 4 + ((chip >> 3) & 1) * 2 + (chip >> 4)


def chip_in(place):
    return (place & 1) * 16 + ((place >> 1) & 1) * 8 + ((place >> 2) & 1) * 4 + (place >> 3)


def open_chip(rows, is_first):
    rows = rows.astype(F32)
    values = jnp.where(is_first, rows[0:16], rows[16:32])
    last = jnp.concatenate([rows[84:88], rows[80:84]], axis=0)
    books = [
        jnp.where(is_first, rows[64:72], rows[72:80]),
        jnp.where(is_first, rows[80:88], last),
    ]
    return values, rows[32:56], rows[56:64], jnp.concatenate(books, axis=0)


def run_and_code(coded):
    run = jnp.zeros_like(coded)
    for bit in range(5, -1, -1):
        over = coded >= 128.0 * 2.0 ** (1 << bit)
        coded = jnp.where(over, coded * 2.0 ** -(1 << bit), coded)
        run = run + jnp.where(over, float(1 << bit), 0.0)
    return run, coded - 128.0


def wide_row(ref, row, size):
    return jnp.broadcast_to(ref[pl.ds(row, 1), :], (size, 128))


def adder(runs, codes, weights, total):
    down = lax.broadcasted_iota(jnp.int32, (16, 128), 0).astype(F32)
    iotas = [(down + 16.0 * step).astype(BF16) for step in range(8)]
    nought = jnp.zeros((16, 128), BF16)
    one = jnp.ones((16, 128), BF16)

    def add_items(section, item_row, source, source_row, count):
        lefts, rights = [], []
        for row in range(count):
            at, source_at = item_row + row, source_row + row
            run = wide_row(runs.at[section], at, 16).astype(BF16)
            code = wide_row(codes.at[section], at, 16).astype(BF16)
            weight = wide_row(weights, at, 16).astype(BF16)
            first = wide_row(source.at[0], source_at, 16).astype(BF16)
            second = wide_row(source.at[1], source_at, 16).astype(BF16)
            masks = [run == iotas[step] for step in range(4)]
            lefts.append(
                jnp.concatenate(
                    [
                        jnp.where(mask, value, nought)
                        for value in (first, second, one)
                        for mask in masks
                    ],
                    axis=0,
                )
            )
            rights.append(
                jnp.concatenate(
                    [jnp.where(code == iotas[step], weight, nought) for step in range(8)], axis=0
                )
            )
        total[...] += lax.dot_general(
            jnp.concatenate(lefts, axis=1),
            jnp.concatenate(rights, axis=1),
            (((1,), (1,)), ((), ())),
            preferred_element_type=F32,
        )

    return add_items


def first_kernel(in_ref, total, runs, codes, weights, residual):
    is_first = lax.axis_index("core") == 0

    @pl.loop(0, CHIPS, unroll=2)
    def _(place):
        at = pl.ds(pl.multiple_of(place * 8, 8), 8)
        values, coded, weight, _ = open_chip(in_ref[place], is_first)
        residual[0, at, :] = values[0:8]
        residual[1, at, :] = values[8:16]
        weights[at, :] = weight
        runs[0, at, :], codes[0, at, :] = run_and_code(coded[0:8])

    add_items = adder(runs, codes, weights, total)
    total[...] = jnp.zeros_like(total)

    @pl.loop(0, CHIPS // 8, unroll=2)
    def _(group):
        add_items(0, group * 64, residual, group * 64, 64)


def sections_kernel(
    in_ref, other_ref, first_ref, out_ref, runs, codes, weights, residual, books_in, books_out, table, total,
    fresh, stage, steps
):
    core = lax.axis_index("core")
    is_first = core == 0

    for half, ref in enumerate((in_ref, other_ref)):

        @pl.loop(0, CHIPS, unroll=2)
        def _(place):
            at = pl.ds(pl.multiple_of((half * CHIPS + place) * 8, 8), 8)
            values, coded, weight, books = open_chip(ref[place], is_first)
            residual[0, at, :] = values[0:8]
            residual[1, at, :] = values[8:16]
            weights[at, :] = weight
            run, code = run_and_code(coded)
            for section in range(SECTIONS):
                runs[section, at, :] = run[section * 8 : section * 8 + 8]
                codes[section, at, :] = code[section * 8 : section * 8 + 8]
            source = chip_in(place) * 2 + (core if half == 0 else 1 - core)
            books_in[pl.ds(pl.multiple_of(source * 16, 16), 16), :] = books

    books_out[...] = jnp.zeros_like(books_out)
    add_items = adder(runs, codes, weights, total)

    def take_block(section, block):
        at = pl.ds(pl.multiple_of(block * 8, 8), 8)
        run = runs[section, at, :]
        code = codes[section, at, :].astype(jnp.int32)
        both = jnp.zeros((8, 128), jnp.int32)
        for each in range(RUNS):
            found = jnp.take_along_axis(
                wide_row(table, each, 8), code, axis=1, mode="promise_in_bounds"
            )
            both = jnp.where(run == float(each), found, both)
        low = (both << 16) >> 16
        result = []
        for which, whole in enumerate(((both - low) >> 16, low)):
            row = whole.astype(F32) * steps[which : which + 1, :]
            left = (residual[which, at, :] - row).astype(BF16)
            residual[which, at, :] = left.astype(F32)
            result.append(left)
        return result

    def update(section):
        weight = total[128:192, :]
        count = prior_weight + weight
        levels = []
        for which in range(2):
            book = jnp.concatenate(
                [
                    books_in[pl.ds(first * 16 + section * 2 + which, 8, stride=16), :]
                    + books_in[pl.ds(first * 16 + 6 + section * 2 + which, 8, stride=16), :]
                    for first in range(0, RUNS, 8)
                ],
                axis=0,
            )
            new = (prior_weight * book + total[which * 64 : which * 64 + 64, :]) / count
            used = jnp.where(weight > 0.0, jnp.abs(new), 0.0)
            largest = jnp.max(jnp.max(used, axis=0, keepdims=True), axis=1, keepdims=True)
            step = jnp.maximum(largest, 1e-20) * (1.0 / 32767.0)
            steps[which : which + 1, :] = jnp.broadcast_to(step, (1, 128))
            level = jnp.clip(new / step, -32767.0, 32767.0)
            levels.append(jnp.round(level).astype(jnp.int32))
            for first in range(0, RUNS, 8):
                books_out[pl.ds(first * 8 + section * 2 + which, 8, stride=8), :] = new[
                    first : first + 8
                ]
        table[...] = levels[0] * 65536 + levels[1]
        total[...] = jnp.zeros_like(total)

    total[...] = first_ref[...]

    @pl.loop(CHIPS // 8, BLOCKS // 8, unroll=2)
    def _(group):
        add_items(0, group * 64, residual, group * 64, 64)

    update(0)
    for section in range(1, SECTIONS):

        def take(group, step):
            left = take_block(section - 1, group * GROUP + step)
            for which in range(2):
                fresh[which, 8 * step : 8 * step + 8, :] = left[which].astype(F32)

        for step in range(GROUP):
            take(0, step)

        @pl.loop(1, BLOCKS // GROUP)
        def _(group):
            stage[...] = fresh[...]
            for step in range(GROUP):
                take(group, step)
                add_items(section, ((group - 1) * GROUP + step) * 8, stage, 8 * step, 8)

        add_items(section, (BLOCKS - GROUP) * 8, fresh, 0, 8 * GROUP)
        update(section)

    for half in range(2):

        @pl.loop(0, CHIPS, unroll=8)
        def _(place):
            left = take_block(SECTIONS - 1, half * CHIPS + place)
            source = chip_in(place) * 2 + (core if half == 0 else 1 - core)
            books = books_out[pl.ds(pl.multiple_of(source * 8, 8), 8), :]
            rows = [left[0].astype(F32), left[1].astype(F32), books]
            out_ref[source] = jnp.concatenate(rows, axis=0).astype(BF16)


def error_kernel(in_ref, error_ref):
    def add(source, error):
        rows = in_ref[source].astype(F32)
        return error + rows[0:8] * rows[0:8] + rows[8:16] * rows[8:16]

    error_ref[...] = lax.fori_loop(0, RUNS, add, jnp.zeros((8, 128), F32), unroll=8)


def unpack_kernel(in_ref, book_ref, left_ref, left_rows, book_rows):
    @pl.loop(0, RUNS, unroll=8)
    def _(source):
        rows = in_ref[source].astype(F32)
        left_rows[pl.ds(pl.multiple_of(source * 16, 16), 16), :] = rows[0:16]
        book_rows[pl.ds(pl.multiple_of(source * 8, 8), 8), :] = rows[16:24]

    for block in range(8):
        turned = jnp.concatenate(
            [
                left_rows[pl.ds(first * 16 + which * 8 + block, 8, stride=16), :]
                for which in range(2)
                for first in range(0, RUNS, 8)
            ],
            axis=0,
        )
        left_ref[block * 128 : (block + 1) * 128, :] = turned.T.astype(BF16)
    for section in range(SECTIONS):
        turned = jnp.concatenate(
            [
                book_rows[pl.ds(first * 8 + section * 2 + which, 8, stride=8), :]
                for which in range(2)
                for first in range(0, RUNS, 8)
            ],
            axis=0,
        )
        book_ref[section] = turned.T


def sum_over_feat(value):
    one, two, three = [
        lax.ppermute(value, "feat", [(at, (at + step) % 4) for at in range(4)])
        for step in range(1, 4)
    ]
    return (value + two) + (one + three)


def per_device(embeddings, code_ids, codebooks, item_weight):
    params = pltpu.CompilerParams(vmem_limit_bytes=48 * 1024 * 1024)
    with jax.named_scope("pack"):
        packed = pl.pallas_call(
            pack_kernel,
            out_shape=jax.ShapeDtypeStruct((CHIPS, ROWS_IN, 128), BF16),
            in_specs=[pl.BlockSpec(memory_space=pltpu.HBM)] * 4,
            scratch_shapes=[
                pltpu.VMEM((1024, FEATS), BF16),
                pltpu.VMEM((SECTIONS, 1024), jnp.int32),
                pltpu.VMEM((8, 128), BF16),
                pltpu.VMEM((SECTIONS, 128, FEATS), F32),
                pltpu.VMEM((RUNS * 16, 128), F32),
                pltpu.VMEM((RUNS * 16, 128), F32),
                pltpu.VMEM((32, 128), F32),
                pltpu.SemaphoreType.DMA((4,)),
            ],
            compiler_params=pltpu.CompilerParams(vmem_limit_bytes=63 * 1024 * 1024),
        )(embeddings, code_ids, item_weight.reshape(8, 128), codebooks)
    with jax.named_scope("to_features"):
        mine = lax.all_to_all(packed, CHIP_PLACES, 0, 0, tiled=True)
    with jax.named_scope("to_other_core"):
        other = lax.ppermute(mine, "core", [(0, 1), (1, 0)])
    with jax.named_scope("first_sums"):
        first = pl.pallas_call(
            first_kernel,
            out_shape=jax.ShapeDtypeStruct((3 * RUNS, 128), F32),
            scratch_shapes=[
                pltpu.VMEM((1, CHIPS * 8, 128), F32),
                pltpu.VMEM((1, CHIPS * 8, 128), F32),
                pltpu.VMEM((CHIPS * 8, 128), F32),
                pltpu.VMEM((2, CHIPS * 8, 128), F32),
            ],
            compiler_params=params,
            cost_estimate=pl.CostEstimate(
                flops=2 * 3 * RUNS * 128 * CHIPS * 1024, bytes_accessed=2**20, transcendentals=0
            ),
        )(mine)
    with jax.named_scope("sections"):
        done = pl.pallas_call(
            sections_kernel,
            out_shape=jax.ShapeDtypeStruct((BLOCKS, ROWS_OUT, 128), BF16),
            scratch_shapes=[
                pltpu.VMEM((SECTIONS, BLOCKS * 8, 128), F32),
                pltpu.VMEM((SECTIONS, BLOCKS * 8, 128), F32),
                pltpu.VMEM((BLOCKS * 8, 128), F32),
                pltpu.VMEM((2, BLOCKS * 8, 128), F32),
                pltpu.VMEM((RUNS * 16, 128), F32),
                pltpu.VMEM((RUNS * 8, 128), F32),
                pltpu.VMEM((RUNS, 128), jnp.int32),
                pltpu.VMEM((3 * RUNS, 128), F32),
                pltpu.VMEM((2, 8 * GROUP, 128), F32),
                pltpu.VMEM((2, 8 * GROUP, 128), F32),
                pltpu.VMEM((8, 128), F32),
            ],
            compiler_params=params,
        )(mine, other, first)
    with jax.named_scope("to_items"):
        back = lax.all_to_all(done, DP, 0, 0, tiled=True)
    with jax.named_scope("error"):
        error = pl.pallas_call(
            error_kernel, out_shape=jax.ShapeDtypeStruct((8, 128), F32), compiler_params=params
        )(back)
        item_error = sum_over_feat(error).reshape(1024)
    with jax.named_scope("unpack"):
        updated, left = pl.pallas_call(
            unpack_kernel,
            out_shape=(
                jax.ShapeDtypeStruct((SECTIONS, 128, FEATS), F32),
                jax.ShapeDtypeStruct((1024, FEATS), BF16),
            ),
            scratch_shapes=[
                pltpu.VMEM((RUNS * 16, 128), F32),
                pltpu.VMEM((RUNS * 8, 128), F32),
            ],
            compiler_params=params,
        )(back)
    return updated, left, item_error


def solution(mesh):
    feat = mesh.devices.shape[1]
    split = Mesh(mesh.devices.reshape(2, 2, 2, 4, 2, feat), (*DP, "feat"))
    in_specs = (P(DP, "feat"), P(None, DP), P(None, DP, "feat"), P(DP))
    out_specs = (P(None, DP, "feat"), P(DP, "feat"), P(DP))
    return jax.shard_map(
        per_device, mesh=split, in_specs=in_specs, out_specs=out_specs, check_vma=False
    )
```

```python
import jax
import jax.numpy as jnp
from jax import lax
from jax.experimental import pallas as pl
from jax.experimental.pallas import tpu as pltpu
from jax.sharding import Mesh
from jax.sharding import PartitionSpec as P

F32 = jnp.float32
BF16 = jnp.bfloat16
SECTIONS = 3
RUNS = 64
BLOCKS = 64
FEATS = 128
prior_weight = 4.0
GROUP = 8

CHIPS = 32
ROWS_IN = 88
ROWS_OUT = 24


def two_parts(x):
    head = x.astype(BF16).astype(F32)
    return head, x - head


def pack_kernel(
    emb_hbm, ids_hbm, w_hbm, book_hbm, out_ref, emb_ref, ids_ref, w_ref, book_ref, emb_rows, book_rows,
    shared_rows, sems
):
    pairs = ((ids_hbm, ids_ref), (w_hbm, w_ref), (emb_hbm, emb_ref), (book_hbm, book_ref))
    copies = [
        pltpu.make_async_copy(source, target, sems.at[at])
        for at, (source, target) in enumerate(pairs)
    ]
    for copy in copies:
        copy.start()
    book_rows[...] = jnp.zeros_like(book_rows)
    copies[0].wait()
    ids = ids_ref[...]
    run = ids >> 7
    coded = ((ids & 127) + 128).astype(F32)
    for bit in range(6):
        coded = coded * jnp.where((run >> bit) & 1 == 1, 2.0 ** (1 << bit), 1.0)
    for block in range(8):
        shared_rows[pl.ds(block, SECTIONS, stride=8), :] = coded[:, block * 128 : block * 128 + 128]
    copies[1].wait()
    shared_rows[24:32, :] = w_ref[...].astype(F32)
    copies[2].wait()
    for block in range(8):
        turned = emb_ref[block * 128 : (block + 1) * 128, :].astype(F32).T
        for group in range(16):
            which, first = group // 8, (group % 8) * 8
            emb_rows[pl.ds(first * 16 + which * 8 + block, 8, stride=16), :] = turned[
                group * 8 : (group + 1) * 8
            ]
    copies[3].wait()
    for section in range(SECTIONS):
        parts = two_parts(book_ref[section].T)
        for part in range(2):
            for group in range(16):
                which, first = group // 8, (group % 8) * 8
                book_rows[
                    pl.ds(first * 16 + part * 6 + section * 2 + which, 8, stride=16), :
                ] = parts[part][group * 8 : (group + 1) * 8]

    shared = shared_rows[...]

    @pl.loop(0, CHIPS, unroll=8)
    def _(chip):
        at = pl.ds(pl.multiple_of(chip * 32, 32), 32)
        books = book_rows[at, :]
        rows = [emb_rows[at, :], shared, books[0:8], books[16:24], books[8:12], books[24:28]]
        out_ref[chip] = jnp.concatenate(rows, axis=0).astype(BF16)


def open_chip(rows, is_first):
    rows = rows.astype(F32)
    values = jnp.where(is_first, rows[0:16], rows[16:32])
    last = jnp.concatenate([rows[84:88], rows[80:84]], axis=0)
    books = [
        jnp.where(is_first, rows[64:72], rows[72:80]),
        jnp.where(is_first, rows[80:88], last),
    ]
    return values, rows[32:56], rows[56:64], jnp.concatenate(books, axis=0)


def run_and_code(coded):
    run = jnp.zeros_like(coded)
    for bit in range(5, -1, -1):
        over = coded >= 128.0 * 2.0 ** (1 << bit)
        coded = jnp.where(over, coded * 2.0 ** -(1 << bit), coded)
        run = run + jnp.where(over, float(1 << bit), 0.0)
    return run, coded - 128.0


def wide_row(ref, row, size):
    return jnp.broadcast_to(ref[pl.ds(row, 1), :], (size, 128))


def adder(runs, codes, weights, total):
    down = lax.broadcasted_iota(jnp.int32, (16, 128), 0).astype(F32)
    iotas = [(down + 16.0 * step).astype(BF16) for step in range(8)]
    nought = jnp.zeros((16, 128), BF16)
    one = jnp.ones((16, 128), BF16)

    def add_items(section, item_row, source, source_row, count):
        lefts, rights = [], []
        for row in range(count):
            at, source_at = item_row + row, source_row + row
            run = wide_row(runs.at[section], at, 16).astype(BF16)
            code = wide_row(codes.at[section], at, 16).astype(BF16)
            weight = wide_row(weights, at, 16).astype(BF16)
            first = wide_row(source.at[0], source_at, 16).astype(BF16)
            second = wide_row(source.at[1], source_at, 16).astype(BF16)
            masks = [run == iotas[step] for step in range(4)]
            lefts.append(
                jnp.concatenate(
                    [
                        jnp.where(mask, value, nought)
                        for value in (first, second, one)
                        for mask in masks
                    ],
                    axis=0,
                )
            )
            rights.append(
                jnp.concatenate(
                    [jnp.where(code == iotas[step], weight, nought) for step in range(8)], axis=0
                )
            )
        total[...] += lax.dot_general(
            jnp.concatenate(lefts, axis=1),
            jnp.concatenate(rights, axis=1),
            (((1,), (1,)), ((), ())),
            preferred_element_type=F32,
        )

    return add_items


def first_kernel(in_ref, total, runs, codes, weights, residual):
    is_first = lax.axis_index("core") == 0

    @pl.loop(0, CHIPS, unroll=8)
    def _(chip):
        at = pl.ds(pl.multiple_of(chip * 8, 8), 8)
        values, coded, weight, _ = open_chip(in_ref[chip], is_first)
        residual[0, at, :] = values[0:8]
        residual[1, at, :] = values[8:16]
        weights[at, :] = weight
        runs[0, at, :], codes[0, at, :] = run_and_code(coded[0:8])

    add_items = adder(runs, codes, weights, total)
    total[...] = jnp.zeros_like(total)

    @pl.loop(0, CHIPS // 8, unroll=2)
    def _(group):
        add_items(0, group * 64, residual, group * 64, 64)


def sections_kernel(
    in_ref, other_ref, first_ref, out_ref, runs, codes, weights, residual, books_in, books_out, table, total,
    fresh, stage, steps
):
    core = lax.axis_index("core")
    is_first = core == 0

    for half, ref in enumerate((in_ref, other_ref)):

        @pl.loop(0, CHIPS, unroll=8)
        def _(chip):
            at = pl.ds(pl.multiple_of((half * CHIPS + chip) * 8, 8), 8)
            values, coded, weight, books = open_chip(ref[chip], is_first)
            residual[0, at, :] = values[0:8]
            residual[1, at, :] = values[8:16]
            weights[at, :] = weight
            run, code = run_and_code(coded)
            for section in range(SECTIONS):
                runs[section, at, :] = run[section * 8 : section * 8 + 8]
                codes[section, at, :] = code[section * 8 : section * 8 + 8]
            source = chip * 2 + (core if half == 0 else 1 - core)
            books_in[pl.ds(pl.multiple_of(source * 16, 16), 16), :] = books

    books_out[...] = jnp.zeros_like(books_out)
    add_items = adder(runs, codes, weights, total)

    def take_block(section, block):
        at = pl.ds(pl.multiple_of(block * 8, 8), 8)
        run = runs[section, at, :]
        code = codes[section, at, :].astype(jnp.int32)
        both = jnp.zeros((8, 128), jnp.int32)
        for each in range(RUNS):
            found = jnp.take_along_axis(
                wide_row(table, each, 8), code, axis=1, mode="promise_in_bounds"
            )
            both = jnp.where(run == float(each), found, both)
        low = (both << 16) >> 16
        result = []
        for which, whole in enumerate(((both - low) >> 16, low)):
            row = whole.astype(F32) * steps[which : which + 1, :]
            left = (residual[which, at, :] - row).astype(BF16)
            residual[which, at, :] = left.astype(F32)
            result.append(left)
        return result

    def update(section):
        weight = total[128:192, :]
        count = prior_weight + weight
        levels = []
        for which in range(2):
            book = jnp.concatenate(
                [
                    books_in[pl.ds(first * 16 + section * 2 + which, 8, stride=16), :]
                    + books_in[pl.ds(first * 16 + 6 + section * 2 + which, 8, stride=16), :]
                    for first in range(0, RUNS, 8)
                ],
                axis=0,
            )
            new = (prior_weight * book + total[which * 64 : which * 64 + 64, :]) / count
            used = jnp.where(weight > 0.0, jnp.abs(new), 0.0)
            largest = jnp.max(jnp.max(used, axis=0, keepdims=True), axis=1, keepdims=True)
            step = jnp.maximum(largest, 1e-20) * (1.0 / 32767.0)
            steps[which : which + 1, :] = jnp.broadcast_to(step, (1, 128))
            level = jnp.clip(new / step, -32767.0, 32767.0)
            levels.append(jnp.round(level).astype(jnp.int32))
            for first in range(0, RUNS, 8):
                books_out[pl.ds(first * 8 + section * 2 + which, 8, stride=8), :] = new[
                    first : first + 8
                ]
        table[...] = levels[0] * 65536 + levels[1]
        total[...] = jnp.zeros_like(total)

    total[...] = first_ref[...]

    @pl.loop(CHIPS // 8, BLOCKS // 8, unroll=2)
    def _(group):
        add_items(0, group * 64, residual, group * 64, 64)

    update(0)
    for section in range(1, SECTIONS):

        def take(group, step):
            left = take_block(section - 1, group * GROUP + step)
            for which in range(2):
                fresh[which, 8 * step : 8 * step + 8, :] = left[which].astype(F32)

        for step in range(GROUP):
            take(0, step)

        @pl.loop(1, BLOCKS // GROUP)
        def _(group):
            stage[...] = fresh[...]
            for step in range(GROUP):
                take(group, step)
                add_items(section, ((group - 1) * GROUP + step) * 8, stage, 8 * step, 8)

        add_items(section, (BLOCKS - GROUP) * 8, fresh, 0, 8 * GROUP)
        update(section)

    for half in range(2):

        @pl.loop(0, CHIPS, unroll=8)
        def _(chip):
            left = take_block(SECTIONS - 1, half * CHIPS + chip)
            source = chip * 2 + (core if half == 0 else 1 - core)
            books = books_out[pl.ds(pl.multiple_of(source * 8, 8), 8), :]
            rows = [left[0].astype(F32), left[1].astype(F32), books]
            out_ref[source] = jnp.concatenate(rows, axis=0).astype(BF16)


def error_kernel(in_ref, error_ref):
    def add(source, error):
        rows = in_ref[source].astype(F32)
        return error + rows[0:8] * rows[0:8] + rows[8:16] * rows[8:16]

    error_ref[...] = lax.fori_loop(0, RUNS, add, jnp.zeros((8, 128), F32), unroll=8)


def unpack_kernel(in_ref, book_ref, left_ref, left_rows, book_rows):
    @pl.loop(0, RUNS, unroll=8)
    def _(source):
        rows = in_ref[source].astype(F32)
        left_rows[pl.ds(pl.multiple_of(source * 16, 16), 16), :] = rows[0:16]
        book_rows[pl.ds(pl.multiple_of(source * 8, 8), 8), :] = rows[16:24]

    for block in range(8):
        turned = jnp.concatenate(
            [
                left_rows[pl.ds(first * 16 + which * 8 + block, 8, stride=16), :]
                for which in range(2)
                for first in range(0, RUNS, 8)
            ],
            axis=0,
        )
        left_ref[block * 128 : (block + 1) * 128, :] = turned.T.astype(BF16)
    for section in range(SECTIONS):
        turned = jnp.concatenate(
            [
                book_rows[pl.ds(first * 8 + section * 2 + which, 8, stride=8), :]
                for which in range(2)
                for first in range(0, RUNS, 8)
            ],
            axis=0,
        )
        book_ref[section] = turned.T


def sum_kernel(value_ref, one_ref, two_ref, three_ref, out_ref):
    out_ref[...] = (value_ref[...] + two_ref[...]) + (one_ref[...] + three_ref[...])


def sum_over_feat(value, params):
    one, two, three = [
        lax.ppermute(value, "feat", [(at, (at + step) % 4) for at in range(4)])
        for step in range(1, 4)
    ]
    return pl.pallas_call(
        sum_kernel, out_shape=jax.ShapeDtypeStruct(value.shape, F32), compiler_params=params
    )(value, one, two, three)


def per_device(embeddings, code_ids, codebooks, item_weight):
    params = pltpu.CompilerParams(vmem_limit_bytes=48 * 1024 * 1024)
    with jax.named_scope("pack"):
        packed = pl.pallas_call(
            pack_kernel,
            out_shape=jax.ShapeDtypeStruct((CHIPS, ROWS_IN, 128), BF16),
            in_specs=[pl.BlockSpec(memory_space=pltpu.HBM)] * 4,
            scratch_shapes=[
                pltpu.VMEM((1024, FEATS), BF16),
                pltpu.VMEM((SECTIONS, 1024), jnp.int32),
                pltpu.VMEM((8, 128), BF16),
                pltpu.VMEM((SECTIONS, 128, FEATS), F32),
                pltpu.VMEM((RUNS * 16, 128), F32),
                pltpu.VMEM((RUNS * 16, 128), F32),
                pltpu.VMEM((32, 128), F32),
                pltpu.SemaphoreType.DMA((4,)),
            ],
            compiler_params=pltpu.CompilerParams(vmem_limit_bytes=63 * 1024 * 1024),
        )(embeddings, code_ids, item_weight.reshape(8, 128), codebooks)
    with jax.named_scope("to_features"):
        mine = lax.all_to_all(packed, "chip", 0, 0, tiled=True)
    with jax.named_scope("to_other_core"):
        other = lax.ppermute(mine, "core", [(0, 1), (1, 0)])
    with jax.named_scope("first_sums"):
        first = pl.pallas_call(
            first_kernel,
            out_shape=jax.ShapeDtypeStruct((3 * RUNS, 128), F32),
            scratch_shapes=[
                pltpu.VMEM((1, CHIPS * 8, 128), F32),
                pltpu.VMEM((1, CHIPS * 8, 128), F32),
                pltpu.VMEM((CHIPS * 8, 128), F32),
                pltpu.VMEM((2, CHIPS * 8, 128), F32),
            ],
            compiler_params=params,
            cost_estimate=pl.CostEstimate(
                flops=2 * 3 * RUNS * 128 * CHIPS * 1024, bytes_accessed=2**20, transcendentals=0
            ),
        )(mine)
    with jax.named_scope("sections"):
        done = pl.pallas_call(
            sections_kernel,
            out_shape=jax.ShapeDtypeStruct((BLOCKS, ROWS_OUT, 128), BF16),
            scratch_shapes=[
                pltpu.VMEM((SECTIONS, BLOCKS * 8, 128), F32),
                pltpu.VMEM((SECTIONS, BLOCKS * 8, 128), F32),
                pltpu.VMEM((BLOCKS * 8, 128), F32),
                pltpu.VMEM((2, BLOCKS * 8, 128), F32),
                pltpu.VMEM((RUNS * 16, 128), F32),
                pltpu.VMEM((RUNS * 8, 128), F32),
                pltpu.VMEM((RUNS, 128), jnp.int32),
                pltpu.VMEM((3 * RUNS, 128), F32),
                pltpu.VMEM((2, 8 * GROUP, 128), F32),
                pltpu.VMEM((2, 8 * GROUP, 128), F32),
                pltpu.VMEM((8, 128), F32),
            ],
            compiler_params=params,
        )(mine, other, first)
    with jax.named_scope("to_items"):
        back = lax.all_to_all(done, ("chip", "core"), 0, 0, tiled=True)
    with jax.named_scope("error"):
        error = pl.pallas_call(
            error_kernel, out_shape=jax.ShapeDtypeStruct((8, 128), F32), compiler_params=params
        )(back)
        item_error = sum_over_feat(error, params).reshape(1024)
    with jax.named_scope("unpack"):
        updated, left = pl.pallas_call(
            unpack_kernel,
            out_shape=(
                jax.ShapeDtypeStruct((SECTIONS, 128, FEATS), F32),
                jax.ShapeDtypeStruct((1024, FEATS), BF16),
            ),
            scratch_shapes=[
                pltpu.VMEM((RUNS * 16, 128), F32),
                pltpu.VMEM((RUNS * 8, 128), F32),
            ],
            compiler_params=params,
        )(back)
    return updated, left, item_error


def solution(mesh):
    dp, feat = mesh.devices.shape
    split = Mesh(mesh.devices.reshape(dp // 2, 2, feat), ("chip", "core", "feat"))
    dp_axes = ("chip", "core")
    in_specs = (P(dp_axes, "feat"), P(None, dp_axes), P(None, dp_axes, "feat"), P(dp_axes))
    out_specs = (P(None, dp_axes, "feat"), P(dp_axes, "feat"), P(dp_axes))
    return jax.shard_map(
        per_device, mesh=split, in_specs=in_specs, out_specs=out_specs, check_vma=False
    )
```

```python
import jax
import jax.numpy as jnp
from jax import lax
from jax.experimental import pallas as pl
from jax.experimental.pallas import tpu as pltpu
from jax.sharding import Mesh
from jax.sharding import PartitionSpec as P

F32 = jnp.float32
BF16 = jnp.bfloat16
SECTIONS = 3
RUNS = 64
BLOCKS = 64
FEATS = 128
prior_weight = 4.0
GROUP = 16

CHIPS = 32
ROWS_IN = 88
ROWS_OUT = 24


def two_parts(x):
    head = x.astype(BF16).astype(F32)
    return head, x - head


def pack_kernel(
    emb_hbm, ids_hbm, w_hbm, book_hbm, out_ref, emb_ref, ids_ref, w_ref, book_ref, emb_rows, book_rows,
    shared_rows, sems
):
    pairs = ((ids_hbm, ids_ref), (w_hbm, w_ref), (emb_hbm, emb_ref), (book_hbm, book_ref))
    copies = [
        pltpu.make_async_copy(source, target, sems.at[at])
        for at, (source, target) in enumerate(pairs)
    ]
    for copy in copies:
        copy.start()
    book_rows[...] = jnp.zeros_like(book_rows)
    copies[0].wait()
    ids = ids_ref[...]
    run = ids >> 7
    coded = ((ids & 127) + 128).astype(F32)
    for bit in range(6):
        coded = coded * jnp.where((run >> bit) & 1 == 1, 2.0 ** (1 << bit), 1.0)
    for block in range(8):
        shared_rows[pl.ds(block, SECTIONS, stride=8), :] = coded[:, block * 128 : block * 128 + 128]
    copies[1].wait()
    shared_rows[24:32, :] = w_ref[...].astype(F32)
    copies[2].wait()
    for block in range(8):
        turned = emb_ref[block * 128 : (block + 1) * 128, :].astype(F32).T
        for group in range(16):
            which, first = group // 8, (group % 8) * 8
            emb_rows[pl.ds(first * 16 + which * 8 + block, 8, stride=16), :] = turned[
                group * 8 : (group + 1) * 8
            ]
    copies[3].wait()
    for section in range(SECTIONS):
        parts = two_parts(book_ref[section].T)
        for part in range(2):
            for group in range(16):
                which, first = group // 8, (group % 8) * 8
                book_rows[
                    pl.ds(first * 16 + part * 6 + section * 2 + which, 8, stride=16), :
                ] = parts[part][group * 8 : (group + 1) * 8]

    shared = shared_rows[...]

    @pl.loop(0, CHIPS, unroll=8)
    def _(chip):
        at = pl.ds(pl.multiple_of(chip * 32, 32), 32)
        books = book_rows[at, :]
        rows = [emb_rows[at, :], shared, books[0:8], books[16:24], books[8:12], books[24:28]]
        out_ref[chip] = jnp.concatenate(rows, axis=0).astype(BF16)


def open_chip(rows, is_first):
    rows = rows.astype(F32)
    values = jnp.where(is_first, rows[0:16], rows[16:32])
    last = jnp.concatenate([rows[84:88], rows[80:84]], axis=0)
    books = [
        jnp.where(is_first, rows[64:72], rows[72:80]),
        jnp.where(is_first, rows[80:88], last),
    ]
    return values, rows[32:56], rows[56:64], jnp.concatenate(books, axis=0)


def run_and_code(coded):
    run = jnp.zeros_like(coded)
    for bit in range(5, -1, -1):
        over = coded >= 128.0 * 2.0 ** (1 << bit)
        coded = jnp.where(over, coded * 2.0 ** -(1 << bit), coded)
        run = run + jnp.where(over, float(1 << bit), 0.0)
    return run, coded - 128.0


def wide_row(ref, row, size):
    return jnp.broadcast_to(ref[pl.ds(row, 1), :], (size, 128))


def adder(runs, codes, weights, total):
    down = lax.broadcasted_iota(jnp.int32, (16, 128), 0).astype(F32)
    iotas = [(down + 16.0 * step).astype(BF16) for step in range(8)]
    nought = jnp.zeros((16, 128), BF16)
    one = jnp.ones((16, 128), BF16)

    def add_items(section, item_row, source, source_row, count):
        lefts, rights = [], []
        for row in range(count):
            at, source_at = item_row + row, source_row + row
            run = wide_row(runs.at[section], at, 16).astype(BF16)
            code = wide_row(codes.at[section], at, 16).astype(BF16)
            weight = wide_row(weights, at, 16).astype(BF16)
            first = wide_row(source.at[0], source_at, 16).astype(BF16)
            second = wide_row(source.at[1], source_at, 16).astype(BF16)
            masks = [run == iotas[step] for step in range(4)]
            lefts.append(
                jnp.concatenate(
                    [
                        jnp.where(mask, value, nought)
                        for value in (first, second, one)
                        for mask in masks
                    ],
                    axis=0,
                )
            )
            rights.append(
                jnp.concatenate(
                    [jnp.where(code == iotas[step], weight, nought) for step in range(8)], axis=0
                )
            )
        total[...] += lax.dot_general(
            jnp.concatenate(lefts, axis=1),
            jnp.concatenate(rights, axis=1),
            (((1,), (1,)), ((), ())),
            preferred_element_type=F32,
        )

    return add_items


def first_kernel(in_ref, total, runs, codes, weights, residual):
    is_first = lax.axis_index("core") == 0

    @pl.loop(0, CHIPS, unroll=8)
    def _(chip):
        at = pl.ds(pl.multiple_of(chip * 8, 8), 8)
        values, coded, weight, _ = open_chip(in_ref[chip], is_first)
        residual[0, at, :] = values[0:8]
        residual[1, at, :] = values[8:16]
        weights[at, :] = weight
        runs[0, at, :], codes[0, at, :] = run_and_code(coded[0:8])

    add_items = adder(runs, codes, weights, total)
    total[...] = jnp.zeros_like(total)

    @pl.loop(0, CHIPS // 8, unroll=2)
    def _(group):
        add_items(0, group * 64, residual, group * 64, 64)


def sections_kernel(
    in_ref, other_ref, first_ref, out_ref, runs, codes, weights, residual, books_in, books_out, table, total,
    fresh, stage, steps
):
    core = lax.axis_index("core")
    is_first = core == 0

    for half, ref in enumerate((in_ref, other_ref)):

        @pl.loop(0, CHIPS, unroll=8)
        def _(chip):
            at = pl.ds(pl.multiple_of((half * CHIPS + chip) * 8, 8), 8)
            values, coded, weight, books = open_chip(ref[chip], is_first)
            residual[0, at, :] = values[0:8]
            residual[1, at, :] = values[8:16]
            weights[at, :] = weight
            run, code = run_and_code(coded)
            for section in range(SECTIONS):
                runs[section, at, :] = run[section * 8 : section * 8 + 8]
                codes[section, at, :] = code[section * 8 : section * 8 + 8]
            source = chip * 2 + (core if half == 0 else 1 - core)
            books_in[pl.ds(pl.multiple_of(source * 16, 16), 16), :] = books

    books_out[...] = jnp.zeros_like(books_out)
    add_items = adder(runs, codes, weights, total)

    def take_block(section, block):
        at = pl.ds(pl.multiple_of(block * 8, 8), 8)
        run = runs[section, at, :]
        code = codes[section, at, :].astype(jnp.int32)
        both = jnp.zeros((8, 128), jnp.int32)
        for each in range(RUNS):
            found = jnp.take_along_axis(
                wide_row(table, each, 8), code, axis=1, mode="promise_in_bounds"
            )
            both = jnp.where(run == float(each), found, both)
        low = (both << 16) >> 16
        result = []
        for which, whole in enumerate(((both - low) >> 16, low)):
            row = whole.astype(F32) * steps[which : which + 1, :]
            left = (residual[which, at, :] - row).astype(BF16)
            residual[which, at, :] = left.astype(F32)
            result.append(left)
        return result

    def update(section):
        weight = total[128:192, :]
        count = prior_weight + weight
        levels = []
        for which in range(2):
            book = jnp.concatenate(
                [
                    books_in[pl.ds(first * 16 + section * 2 + which, 8, stride=16), :]
                    + books_in[pl.ds(first * 16 + 6 + section * 2 + which, 8, stride=16), :]
                    for first in range(0, RUNS, 8)
                ],
                axis=0,
            )
            new = (prior_weight * book + total[which * 64 : which * 64 + 64, :]) / count
            used = jnp.where(weight > 0.0, jnp.abs(new), 0.0)
            largest = jnp.max(jnp.max(used, axis=0, keepdims=True), axis=1, keepdims=True)
            step = jnp.maximum(largest, 1e-20) * (1.0 / 32767.0)
            steps[which : which + 1, :] = jnp.broadcast_to(step, (1, 128))
            level = jnp.clip(new / step, -32767.0, 32767.0)
            levels.append(jnp.round(level).astype(jnp.int32))
            for first in range(0, RUNS, 8):
                books_out[pl.ds(first * 8 + section * 2 + which, 8, stride=8), :] = new[
                    first : first + 8
                ]
        table[...] = levels[0] * 65536 + levels[1]
        total[...] = jnp.zeros_like(total)

    total[...] = first_ref[...]

    @pl.loop(CHIPS // 8, BLOCKS // 8, unroll=2)
    def _(group):
        add_items(0, group * 64, residual, group * 64, 64)

    update(0)
    for section in range(1, SECTIONS):

        def take(group, step):
            left = take_block(section - 1, group * GROUP + step)
            for which in range(2):
                fresh[which, 8 * step : 8 * step + 8, :] = left[which].astype(F32)

        for step in range(GROUP):
            take(0, step)

        @pl.loop(1, BLOCKS // GROUP)
        def _(group):
            stage[...] = fresh[...]
            for step in range(GROUP):
                take(group, step)
                add_items(section, ((group - 1) * GROUP + step) * 8, stage, 8 * step, 8)

        add_items(section, (BLOCKS - GROUP) * 8, fresh, 0, 8 * GROUP)
        update(section)

    for half in range(2):

        @pl.loop(0, CHIPS, unroll=8)
        def _(chip):
            left = take_block(SECTIONS - 1, half * CHIPS + chip)
            source = chip * 2 + (core if half == 0 else 1 - core)
            books = books_out[pl.ds(pl.multiple_of(source * 8, 8), 8), :]
            rows = [left[0].astype(F32), left[1].astype(F32), books]
            out_ref[source] = jnp.concatenate(rows, axis=0).astype(BF16)


def error_kernel(in_ref, error_ref):
    def add(source, error):
        rows = in_ref[source].astype(F32)
        return error + rows[0:8] * rows[0:8] + rows[8:16] * rows[8:16]

    error_ref[...] = lax.fori_loop(0, RUNS, add, jnp.zeros((8, 128), F32), unroll=8)


def unpack_kernel(in_ref, book_ref, left_ref, left_rows, book_rows):
    @pl.loop(0, RUNS, unroll=8)
    def _(source):
        rows = in_ref[source].astype(F32)
        left_rows[pl.ds(pl.multiple_of(source * 16, 16), 16), :] = rows[0:16]
        book_rows[pl.ds(pl.multiple_of(source * 8, 8), 8), :] = rows[16:24]

    for block in range(8):
        turned = jnp.concatenate(
            [
                left_rows[pl.ds(first * 16 + which * 8 + block, 8, stride=16), :]
                for which in range(2)
                for first in range(0, RUNS, 8)
            ],
            axis=0,
        )
        left_ref[block * 128 : (block + 1) * 128, :] = turned.T.astype(BF16)
    for section in range(SECTIONS):
        turned = jnp.concatenate(
            [
                book_rows[pl.ds(first * 8 + section * 2 + which, 8, stride=8), :]
                for which in range(2)
                for first in range(0, RUNS, 8)
            ],
            axis=0,
        )
        book_ref[section] = turned.T


def sum_kernel(value_ref, one_ref, two_ref, three_ref, out_ref):
    out_ref[...] = (value_ref[...] + two_ref[...]) + (one_ref[...] + three_ref[...])


def sum_over_feat(value, params):
    one, two, three = [
        lax.ppermute(value, "feat", [(at, (at + step) % 4) for at in range(4)])
        for step in range(1, 4)
    ]
    return pl.pallas_call(
        sum_kernel, out_shape=jax.ShapeDtypeStruct(value.shape, F32), compiler_params=params
    )(value, one, two, three)


def per_device(embeddings, code_ids, codebooks, item_weight):
    params = pltpu.CompilerParams(vmem_limit_bytes=48 * 1024 * 1024)
    with jax.named_scope("pack"):
        packed = pl.pallas_call(
            pack_kernel,
            out_shape=jax.ShapeDtypeStruct((CHIPS, ROWS_IN, 128), BF16),
            in_specs=[pl.BlockSpec(memory_space=pltpu.HBM)] * 4,
            scratch_shapes=[
                pltpu.VMEM((1024, FEATS), BF16),
                pltpu.VMEM((SECTIONS, 1024), jnp.int32),
                pltpu.VMEM((8, 128), BF16),
                pltpu.VMEM((SECTIONS, 128, FEATS), F32),
                pltpu.VMEM((RUNS * 16, 128), F32),
                pltpu.VMEM((RUNS * 16, 128), F32),
                pltpu.VMEM((32, 128), F32),
                pltpu.SemaphoreType.DMA((4,)),
            ],
            compiler_params=pltpu.CompilerParams(vmem_limit_bytes=63 * 1024 * 1024),
        )(embeddings, code_ids, item_weight.reshape(8, 128), codebooks)
    with jax.named_scope("to_features"):
        mine = lax.all_to_all(packed, "chip", 0, 0, tiled=True)
    with jax.named_scope("to_other_core"):
        other = lax.ppermute(mine, "core", [(0, 1), (1, 0)])
    with jax.named_scope("first_sums"):
        first = pl.pallas_call(
            first_kernel,
            out_shape=jax.ShapeDtypeStruct((3 * RUNS, 128), F32),
            scratch_shapes=[
                pltpu.VMEM((1, CHIPS * 8, 128), F32),
                pltpu.VMEM((1, CHIPS * 8, 128), F32),
                pltpu.VMEM((CHIPS * 8, 128), F32),
                pltpu.VMEM((2, CHIPS * 8, 128), F32),
            ],
            compiler_params=params,
            cost_estimate=pl.CostEstimate(
                flops=2 * 3 * RUNS * 128 * CHIPS * 1024, bytes_accessed=2**20, transcendentals=0
            ),
        )(mine)
    with jax.named_scope("sections"):
        done = pl.pallas_call(
            sections_kernel,
            out_shape=jax.ShapeDtypeStruct((BLOCKS, ROWS_OUT, 128), BF16),
            scratch_shapes=[
                pltpu.VMEM((SECTIONS, BLOCKS * 8, 128), F32),
                pltpu.VMEM((SECTIONS, BLOCKS * 8, 128), F32),
                pltpu.VMEM((BLOCKS * 8, 128), F32),
                pltpu.VMEM((2, BLOCKS * 8, 128), F32),
                pltpu.VMEM((RUNS * 16, 128), F32),
                pltpu.VMEM((RUNS * 8, 128), F32),
                pltpu.VMEM((RUNS, 128), jnp.int32),
                pltpu.VMEM((3 * RUNS, 128), F32),
                pltpu.VMEM((2, 8 * GROUP, 128), F32),
                pltpu.VMEM((2, 8 * GROUP, 128), F32),
                pltpu.VMEM((8, 128), F32),
            ],
            compiler_params=params,
        )(mine, other, first)
    with jax.named_scope("to_items"):
        back = lax.all_to_all(done, ("chip", "core"), 0, 0, tiled=True)
    with jax.named_scope("error"):
        error = pl.pallas_call(
            error_kernel, out_shape=jax.ShapeDtypeStruct((8, 128), F32), compiler_params=params
        )(back)
        item_error = sum_over_feat(error, params).reshape(1024)
    with jax.named_scope("unpack"):
        updated, left = pl.pallas_call(
            unpack_kernel,
            out_shape=(
                jax.ShapeDtypeStruct((SECTIONS, 128, FEATS), F32),
                jax.ShapeDtypeStruct((1024, FEATS), BF16),
            ),
            scratch_shapes=[
                pltpu.VMEM((RUNS * 16, 128), F32),
                pltpu.VMEM((RUNS * 8, 128), F32),
            ],
            compiler_params=params,
        )(back)
    return updated, left, item_error


def solution(mesh):
    dp, feat = mesh.devices.shape
    split = Mesh(mesh.devices.reshape(dp // 2, 2, feat), ("chip", "core", "feat"))
    dp_axes = ("chip", "core")
    in_specs = (P(dp_axes, "feat"), P(None, dp_axes), P(None, dp_axes, "feat"), P(dp_axes))
    out_specs = (P(None, dp_axes, "feat"), P(dp_axes, "feat"), P(dp_axes))
    return jax.shard_map(
        per_device, mesh=split, in_specs=in_specs, out_specs=out_specs, check_vma=False
    )
```

```python
import jax
import jax.numpy as jnp
from jax import lax
from jax.experimental import pallas as pl
from jax.experimental.pallas import tpu as pltpu
from jax.sharding import Mesh
from jax.sharding import PartitionSpec as P

F32 = jnp.float32
BF16 = jnp.bfloat16
SECTIONS = 3
RUNS = 64
BLOCKS = 64
FEATS = 128
prior_weight = 4.0
GROUP = 16

CHIPS = 32
ROWS_IN = 88
ROWS_OUT = 24


def two_parts(x):
    head = x.astype(BF16).astype(F32)
    return head, x - head


def pack_kernel(
    emb_hbm, ids_hbm, w_hbm, book_hbm, out_ref, emb_ref, ids_ref, w_ref, book_ref, emb_rows, book_rows,
    shared_rows, sems
):
    pairs = ((ids_hbm, ids_ref), (w_hbm, w_ref), (emb_hbm, emb_ref), (book_hbm, book_ref))
    copies = [
        pltpu.make_async_copy(source, target, sems.at[at])
        for at, (source, target) in enumerate(pairs)
    ]
    for copy in copies:
        copy.start()
    book_rows[...] = jnp.zeros_like(book_rows)
    copies[0].wait()
    ids = ids_ref[...]
    run = ids >> 7
    coded = ((ids & 127) + 128).astype(F32)
    for bit in range(6):
        coded = coded * jnp.where((run >> bit) & 1 == 1, 2.0 ** (1 << bit), 1.0)
    for block in range(8):
        shared_rows[pl.ds(block, SECTIONS, stride=8), :] = coded[:, block * 128 : block * 128 + 128]
    copies[1].wait()
    shared_rows[24:32, :] = w_ref[...].astype(F32)
    copies[2].wait()
    for block in range(8):
        turned = emb_ref[block * 128 : (block + 1) * 128, :].astype(F32).T
        for group in range(16):
            which, first = group // 8, (group % 8) * 8
            emb_rows[pl.ds(first * 16 + which * 8 + block, 8, stride=16), :] = turned[
                group * 8 : (group + 1) * 8
            ]
    copies[3].wait()
    for section in range(SECTIONS):
        parts = two_parts(book_ref[section].T)
        for part in range(2):
            for group in range(16):
                which, first = group // 8, (group % 8) * 8
                book_rows[
                    pl.ds(first * 16 + part * 6 + section * 2 + which, 8, stride=16), :
                ] = parts[part][group * 8 : (group + 1) * 8]

    shared = shared_rows[...]

    @pl.loop(0, CHIPS, unroll=8)
    def _(chip):
        at = pl.ds(pl.multiple_of(chip * 32, 32), 32)
        books = book_rows[at, :]
        rows = [emb_rows[at, :], shared, books[0:8], books[16:24], books[8:12], books[24:28]]
        out_ref[chip] = jnp.concatenate(rows, axis=0).astype(BF16)


def open_chip(rows, is_first):
    rows = rows.astype(F32)
    values = jnp.where(is_first, rows[0:16], rows[16:32])
    last = jnp.concatenate([rows[84:88], rows[80:84]], axis=0)
    books = [
        jnp.where(is_first, rows[64:72], rows[72:80]),
        jnp.where(is_first, rows[80:88], last),
    ]
    return values, rows[32:56], rows[56:64], jnp.concatenate(books, axis=0)


def run_and_code(coded):
    run = jnp.zeros_like(coded)
    for bit in range(5, -1, -1):
        over = coded >= 128.0 * 2.0 ** (1 << bit)
        coded = jnp.where(over, coded * 2.0 ** -(1 << bit), coded)
        run = run + jnp.where(over, float(1 << bit), 0.0)
    return run, coded - 128.0


def wide_row(ref, row, size):
    return jnp.broadcast_to(ref[pl.ds(row, 1), :], (size, 128))


def adder(runs, codes, weights, total):
    down = lax.broadcasted_iota(jnp.int32, (16, 128), 0).astype(F32)
    iotas = [(down + 16.0 * step).astype(BF16) for step in range(8)]
    nought = jnp.zeros((16, 128), BF16)
    one = jnp.ones((16, 128), BF16)

    def add_items(section, item_row, source, source_row, count):
        lefts, rights = [], []
        for row in range(count):
            at, source_at = item_row + row, source_row + row
            run = wide_row(runs.at[section], at, 16).astype(BF16)
            code = wide_row(codes.at[section], at, 16).astype(BF16)
            weight = wide_row(weights, at, 16).astype(BF16)
            first = wide_row(source.at[0], source_at, 16).astype(BF16)
            second = wide_row(source.at[1], source_at, 16).astype(BF16)
            masks = [run == iotas[step] for step in range(4)]
            lefts.append(
                jnp.concatenate(
                    [
                        jnp.where(mask, value, nought)
                        for value in (first, second, one)
                        for mask in masks
                    ],
                    axis=0,
                )
            )
            rights.append(
                jnp.concatenate(
                    [jnp.where(code == iotas[step], weight, nought) for step in range(8)], axis=0
                )
            )
        total[...] += lax.dot_general(
            jnp.concatenate(lefts, axis=1),
            jnp.concatenate(rights, axis=1),
            (((1,), (1,)), ((), ())),
            preferred_element_type=F32,
        )

    return add_items


def first_kernel(in_ref, total, runs, codes, weights, residual):
    is_first = lax.axis_index("core") == 0

    @pl.loop(0, CHIPS, unroll=8)
    def _(chip):
        at = pl.ds(pl.multiple_of(chip * 8, 8), 8)
        values, coded, weight, _ = open_chip(in_ref[chip], is_first)
        residual[0, at, :] = values[0:8]
        residual[1, at, :] = values[8:16]
        weights[at, :] = weight
        runs[0, at, :], codes[0, at, :] = run_and_code(coded[0:8])

    add_items = adder(runs, codes, weights, total)
    total[...] = jnp.zeros_like(total)

    @pl.loop(0, CHIPS // 8, unroll=2)
    def _(group):
        add_items(0, group * 64, residual, group * 64, 64)


def sections_kernel(
    in_ref, other_ref, first_ref, out_ref, runs, codes, weights, residual, books_in, books_out, table, total,
    fresh, stage, steps
):
    core = lax.axis_index("core")
    is_first = core == 0

    for half, ref in enumerate((in_ref, other_ref)):

        @pl.loop(0, CHIPS, unroll=8)
        def _(chip):
            at = pl.ds(pl.multiple_of((half * CHIPS + chip) * 8, 8), 8)
            values, coded, weight, books = open_chip(ref[chip], is_first)
            residual[0, at, :] = values[0:8]
            residual[1, at, :] = values[8:16]
            weights[at, :] = weight
            run, code = run_and_code(coded)
            for section in range(SECTIONS):
                runs[section, at, :] = run[section * 8 : section * 8 + 8]
                codes[section, at, :] = code[section * 8 : section * 8 + 8]
            source = chip * 2 + (core if half == 0 else 1 - core)
            books_in[pl.ds(pl.multiple_of(source * 16, 16), 16), :] = books

    books_out[...] = jnp.zeros_like(books_out)
    add_items = adder(runs, codes, weights, total)

    def take_block(section, block):
        at = pl.ds(pl.multiple_of(block * 8, 8), 8)
        run = runs[section, at, :]
        code = codes[section, at, :].astype(jnp.int32)
        both = jnp.zeros((8, 128), jnp.int32)
        for each in range(RUNS):
            found = jnp.take_along_axis(
                wide_row(table, each, 8), code, axis=1, mode="promise_in_bounds"
            )
            both = jnp.where(run == float(each), found, both)
        low = (both << 16) >> 16
        result = []
        for which, whole in enumerate(((both - low) >> 16, low)):
            row = whole.astype(F32) * steps[which : which + 1, :]
            left = (residual[which, at, :] - row).astype(BF16)
            residual[which, at, :] = left.astype(F32)
            result.append(left)
        return result

    def update(section):
        weight = total[128:192, :]
        count = prior_weight + weight
        levels = []
        for which in range(2):
            book = jnp.concatenate(
                [
                    books_in[pl.ds(first * 16 + section * 2 + which, 8, stride=16), :]
                    + books_in[pl.ds(first * 16 + 6 + section * 2 + which, 8, stride=16), :]
                    for first in range(0, RUNS, 8)
                ],
                axis=0,
            )
            new = (prior_weight * book + total[which * 64 : which * 64 + 64, :]) / count
            used = jnp.where(weight > 0.0, jnp.abs(new), 0.0)
            largest = jnp.max(jnp.max(used, axis=0, keepdims=True), axis=1, keepdims=True)
            step = jnp.maximum(largest, 1e-20) * (1.0 / 32767.0)
            steps[which : which + 1, :] = jnp.broadcast_to(step, (1, 128))
            level = jnp.clip(new / step, -32767.0, 32767.0)
            levels.append(jnp.round(level).astype(jnp.int32))
            for first in range(0, RUNS, 8):
                books_out[pl.ds(first * 8 + section * 2 + which, 8, stride=8), :] = new[
                    first : first + 8
                ]
        table[...] = levels[0] * 65536 + levels[1]
        total[...] = jnp.zeros_like(total)

    total[...] = first_ref[...]

    @pl.loop(CHIPS // 8, BLOCKS // 8, unroll=2)
    def _(group):
        add_items(0, group * 64, residual, group * 64, 64)

    update(0)
    for section in range(1, SECTIONS):

        def take(group, step):
            left = take_block(section - 1, group * GROUP + step)
            for which in range(2):
                fresh[which, 8 * step : 8 * step + 8, :] = left[which].astype(F32)

        for step in range(GROUP):
            take(0, step)

        @pl.loop(1, BLOCKS // GROUP)
        def _(group):
            stage[...] = fresh[...]
            for step in range(GROUP):
                take(group, step)
                add_items(section, ((group - 1) * GROUP + step) * 8, stage, 8 * step, 8)

        add_items(section, (BLOCKS - GROUP) * 8, fresh, 0, 8 * GROUP)
        update(section)

    for half in range(2):

        @pl.loop(0, CHIPS, unroll=8)
        def _(chip):
            left = take_block(SECTIONS - 1, half * CHIPS + chip)
            source = chip * 2 + (core if half == 0 else 1 - core)
            books = books_out[pl.ds(pl.multiple_of(source * 8, 8), 8), :]
            rows = [left[0].astype(F32), left[1].astype(F32), books]
            out_ref[source] = jnp.concatenate(rows, axis=0).astype(BF16)


def error_kernel(in_ref, error_ref):
    def add(source, error):
        rows = in_ref[source].astype(F32)
        return error + rows[0:8] * rows[0:8] + rows[8:16] * rows[8:16]

    error_ref[...] = lax.fori_loop(0, RUNS, add, jnp.zeros((8, 128), F32), unroll=8)


def unpack_kernel(in_ref, book_ref, left_ref, left_rows, book_rows):
    @pl.loop(0, RUNS, unroll=8)
    def _(source):
        rows = in_ref[source].astype(F32)
        left_rows[pl.ds(pl.multiple_of(source * 16, 16), 16), :] = rows[0:16]
        book_rows[pl.ds(pl.multiple_of(source * 8, 8), 8), :] = rows[16:24]

    for block in range(8):
        turned = jnp.concatenate(
            [
                left_rows[pl.ds(first * 16 + which * 8 + block, 8, stride=16), :]
                for which in range(2)
                for first in range(0, RUNS, 8)
            ],
            axis=0,
        )
        left_ref[block * 128 : (block + 1) * 128, :] = turned.T.astype(BF16)
    for section in range(SECTIONS):
        turned = jnp.concatenate(
            [
                book_rows[pl.ds(first * 8 + section * 2 + which, 8, stride=8), :]
                for which in range(2)
                for first in range(0, RUNS, 8)
            ],
            axis=0,
        )
        book_ref[section] = turned.T


def per_device(embeddings, code_ids, codebooks, item_weight):
    params = pltpu.CompilerParams(vmem_limit_bytes=48 * 1024 * 1024)
    with jax.named_scope("pack"):
        packed = pl.pallas_call(
            pack_kernel,
            out_shape=jax.ShapeDtypeStruct((CHIPS, ROWS_IN, 128), BF16),
            in_specs=[pl.BlockSpec(memory_space=pltpu.HBM)] * 4,
            scratch_shapes=[
                pltpu.VMEM((1024, FEATS), BF16),
                pltpu.VMEM((SECTIONS, 1024), jnp.int32),
                pltpu.VMEM((8, 128), BF16),
                pltpu.VMEM((SECTIONS, 128, FEATS), F32),
                pltpu.VMEM((RUNS * 16, 128), F32),
                pltpu.VMEM((RUNS * 16, 128), F32),
                pltpu.VMEM((32, 128), F32),
                pltpu.SemaphoreType.DMA((4,)),
            ],
            compiler_params=pltpu.CompilerParams(vmem_limit_bytes=63 * 1024 * 1024),
        )(embeddings, code_ids, item_weight.reshape(8, 128), codebooks)
    with jax.named_scope("to_features"):
        mine = lax.all_to_all(packed, "chip", 0, 0, tiled=True)
    with jax.named_scope("to_other_core"):
        other = lax.ppermute(mine, "core", [(0, 1), (1, 0)])
    with jax.named_scope("first_sums"):
        first = pl.pallas_call(
            first_kernel,
            out_shape=jax.ShapeDtypeStruct((3 * RUNS, 128), F32),
            scratch_shapes=[
                pltpu.VMEM((1, CHIPS * 8, 128), F32),
                pltpu.VMEM((1, CHIPS * 8, 128), F32),
                pltpu.VMEM((CHIPS * 8, 128), F32),
                pltpu.VMEM((2, CHIPS * 8, 128), F32),
            ],
            compiler_params=params,
            cost_estimate=pl.CostEstimate(
                flops=2 * 3 * RUNS * 128 * CHIPS * 1024, bytes_accessed=2**20, transcendentals=0
            ),
        )(mine)
    with jax.named_scope("sections"):
        done = pl.pallas_call(
            sections_kernel,
            out_shape=jax.ShapeDtypeStruct((BLOCKS, ROWS_OUT, 128), BF16),
            scratch_shapes=[
                pltpu.VMEM((SECTIONS, BLOCKS * 8, 128), F32),
                pltpu.VMEM((SECTIONS, BLOCKS * 8, 128), F32),
                pltpu.VMEM((BLOCKS * 8, 128), F32),
                pltpu.VMEM((2, BLOCKS * 8, 128), F32),
                pltpu.VMEM((RUNS * 16, 128), F32),
                pltpu.VMEM((RUNS * 8, 128), F32),
                pltpu.VMEM((RUNS, 128), jnp.int32),
                pltpu.VMEM((3 * RUNS, 128), F32),
                pltpu.VMEM((2, 8 * GROUP, 128), F32),
                pltpu.VMEM((2, 8 * GROUP, 128), F32),
                pltpu.VMEM((8, 128), F32),
            ],
            compiler_params=params,
        )(mine, other, first)
    with jax.named_scope("to_items"):
        back = lax.all_to_all(done, ("chip", "core"), 0, 0, tiled=True)
    with jax.named_scope("error"):
        error = pl.pallas_call(
            error_kernel, out_shape=jax.ShapeDtypeStruct((8, 128), F32), compiler_params=params
        )(back)
        item_error = lax.psum(error, "feat").reshape(1024)
    with jax.named_scope("unpack"):
        updated, left = pl.pallas_call(
            unpack_kernel,
            out_shape=(
                jax.ShapeDtypeStruct((SECTIONS, 128, FEATS), F32),
                jax.ShapeDtypeStruct((1024, FEATS), BF16),
            ),
            scratch_shapes=[
                pltpu.VMEM((RUNS * 16, 128), F32),
                pltpu.VMEM((RUNS * 8, 128), F32),
            ],
            compiler_params=params,
        )(back)
    return updated, left, item_error


def solution(mesh):
    dp, feat = mesh.devices.shape
    split = Mesh(mesh.devices.reshape(dp // 2, 2, feat), ("chip", "core", "feat"))
    dp_axes = ("chip", "core")
    in_specs = (P(dp_axes, "feat"), P(None, dp_axes), P(None, dp_axes, "feat"), P(dp_axes))
    out_specs = (P(None, dp_axes, "feat"), P(dp_axes, "feat"), P(dp_axes))
    return jax.shard_map(
        per_device, mesh=split, in_specs=in_specs, out_specs=out_specs, check_vma=False
    )
```
